128 devices in a mesh: island: 16 (over y, z_hi, core), fsdp: 8 (over x, z_lo).
Axes of the slice: x: 4, y: 4, z: 4 (z_hi: 2, z_lo: 2; z = z_hi * 2 + z_lo), core: 2. Of those that a mesh axis runs over, the one named last changes fastest.
Arguments:
- tokens: bfloat16 [65536, 2048], P(('island', 'fsdp')), may hold values from -6 to 6
- cotangent: bfloat16 [65536, 2048], P(('island', 'fsdp')), may hold values from -0.09375 to 0.09375
- norm_gain: float32 [16, 2048], P('island'), may hold values from 0.5 to 1.5
- qkv_weight: bfloat16 [16, 2048, 1536], P('island', 'fsdp'), may hold values from -0.125 to 0.125
- out_weight: bfloat16 [16, 1024, 2048], P('island', 'fsdp'), may hold values from -0.1875 to 0.1875
- gain_first: float32 [16, 2048], P('island'), may hold values from -2 to 2
- gain_second: float32 [16, 2048], P('island'), may hold values from 0.01 to 1
- qkv_first: float32 [16, 2048, 1536], P('island', 'fsdp'), may hold values from -2 to 2
- qkv_second: float32 [16, 2048, 1536], P('island', 'fsdp'), may hold values from 0.01 to 1
- out_first: float32 [16, 1024, 2048], P('island', 'fsdp'), may hold values from -2 to 2
- out_second: float32 [16, 1024, 2048], P('island', 'fsdp'), may hold values from 0.01 to 1
- gain_global: float32 [2048], replicated, may hold values from 0.5 to 1.5
- gain_momentum: float32 [2048], replicated, may hold values from -1 to 1
- qkv_global: float32 [2048, 1536], P('fsdp', 'island'), may hold values from -0.125 to 0.125
- qkv_momentum: float32 [2048, 1536], P('fsdp', 'island'), may hold values from -0.1 to 0.1
- out_global: float32 [1024, 2048], P('fsdp', 'island'), may hold values from -0.1875 to 0.1875
- out_momentum: float32 [1024, 2048], P('fsdp', 'island'), may hold values from -0.1 to 0.1
Outputs:
- gain_next: float32 [16, 2048], P('island')
- qkv_next: bfloat16 [16, 2048, 1536], P('island', 'fsdp')
- out_next: bfloat16 [16, 1024, 2048], P('island', 'fsdp')
- gain_first_next: float32 [16, 2048], P('island')
- gain_second_next: float32 [16, 2048], P('island')
- qkv_first_next: float32 [16, 2048, 1536], P('island', 'fsdp')
- qkv_second_next: float32 [16, 2048, 1536], P('island', 'fsdp')
- out_first_next: float32 [16, 1024, 2048], P('island', 'fsdp')
- out_second_next: float32 [16, 1024, 2048], P('island', 'fsdp')
- gain_global_next: float32 [2048], replicated
- gain_momentum_next: float32 [2048], replicated
- qkv_global_next: float32 [2048, 1536], P('fsdp', 'island')
- qkv_momentum_next: float32 [2048, 1536], P('fsdp', 'island')
- out_global_next: float32 [1024, 2048], P('fsdp', 'island')
- out_momentum_next: float32 [1024, 2048], P('fsdp', 'island')
The draws below stay inside these ranges and needn't reach their ends.
All inputs are finite; a program needn't handle non-finite values.
Results may differ from the reference program's by a relative error of at most 0.01.
Values may be sent and summed in bfloat16 or wider, within the bound.
A program may use at most 192 MiB of HBM per device.

```python
import math
import jax
import jax.numpy as jnp
from jax import lax

D = 2048
HEADS = 16
KV_HEADS = 4
HEAD_DIM = 64
TOK_DEV = 512
QW = 1024
QKV = 1536
ISLANDS = 16
TOKENS = 65536
N_ISLAND = 16
N_FSDP = 8


def block_levels(stream_key, extent, shards, least, largest):
    level = 1.0
    for axis_at, parts in shards:
        heights = jax.random.uniform(jax.random.fold_in(jax.random.fold_in(stream_key, 6), axis_at), (parts,), jnp.float32, least / len(shards), largest / len(shards))
        level = level * jnp.repeat(jnp.exp(heights), extent[axis_at] // parts).reshape((-1,) + (1,) * (len(extent) - 1 - axis_at))
    return level


def scatter_about(rng, extent, width, limit, cuts=(), held_as=jnp.bfloat16):
    factor_of = block_levels(rng, extent, cuts, -0.22, 0.18) if cuts else 1.0
    array = jax.random.normal(rng, extent, jnp.float32) * width * factor_of
    return jnp.minimum(jnp.maximum(array, -limit), limit).astype(held_as)


def setup_inputs(seed: int = 0) -> dict:
    splits = jax.random.split(jax.random.key(seed), 18)
    return {
        "tokens": scatter_about(splits[0], (TOKENS, D), 1.0, 6.0, ((0, 128),)),
        "cotangent": scatter_about(splits[1], (TOKENS, D), (TOK_DEV * N_FSDP) ** -0.5, 0.09375, ((0, 128),)),
        "norm_gain": jnp.clip(1.0 + 0.1 * jax.random.normal(splits[2], (ISLANDS, D), jnp.float32), 0.5, 1.5),
        "qkv_weight": scatter_about(splits[3], (ISLANDS, D, QKV), D ** -0.5, 0.125, ((0, 16), (1, 8))),
        "out_weight": scatter_about(splits[4], (ISLANDS, QW, D), QW ** -0.5, 0.1875, ((0, 16), (1, 8))),
        "gain_first": scatter_about(splits[5], (ISLANDS, D), 0.3, 2.0, ((0, 16),), jnp.float32),
        "gain_second": jnp.clip(jnp.exp(math.log(1.0) - 4.6051702 * jax.random.uniform(splits[6], (ISLANDS, D), jnp.float32) ** block_levels(splits[6], (ISLANDS, D), ((0, 16),), -0.2, 0.2)), 0.01, 1.0),
        "qkv_first": scatter_about(splits[7], (ISLANDS, D, QKV), 0.3, 2.0, ((0, 16), (1, 8)), jnp.float32),
        "qkv_second": jnp.clip(jnp.exp(math.log(1.0) - 4.6051702 * jax.random.uniform(splits[8], (ISLANDS, D, QKV), jnp.float32) ** block_levels(splits[8], (ISLANDS, D, QKV), ((0, 16), (1, 8)), -0.2, 0.2)), 0.01, 1.0),
        "out_first": scatter_about(splits[9], (ISLANDS, QW, D), 0.3, 2.0, ((0, 16), (1, 8)), jnp.float32),
        "out_second": jnp.clip(jnp.exp(math.log(1.0) - 4.6051702 * jax.random.uniform(splits[10], (ISLANDS, QW, D), jnp.float32) ** block_levels(splits[10], (ISLANDS, QW, D), ((0, 16), (1, 8)), -0.2, 0.2)), 0.01, 1.0),
        "gain_global": jnp.clip(1.0 + 0.1 * jax.random.normal(splits[11], (D,), jnp.float32), 0.5, 1.5),
        "gain_momentum": scatter_about(splits[12], (D,), 0.1, 1.0, (), jnp.float32),
        "qkv_global": scatter_about(splits[13], (D, QKV), D ** -0.5, 0.125, ((0, 8), (1, 16)), jnp.float32),
        "qkv_momentum": scatter_about(splits[14], (D, QKV), 0.01, 0.1, ((0, 8), (1, 16)), jnp.float32),
        "out_global": scatter_about(splits[15], (QW, D), QW ** -0.5, 0.1875, ((0, 8), (1, 16)), jnp.float32),
        "out_momentum": scatter_about(splits[16], (QW, D), 0.01, 0.1, ((0, 8), (1, 16)), jnp.float32),
    }


BETA_ONE = 0.9
BETA_TWO = 0.95
ADAM_EPS = 1e-08
INNER_RATE = 0.001
WEIGHT_DECAY = 0.1
STEP_COUNT = 100.0
OUTER_RATE = 0.7
OUTER_MOMENTUM = 0.9
MIXING = 0.5
NORM_EPS = 1e-05
ROPE_BASE = 500000.0

def rotary(heads, positions):
    half = heads.shape[-1] // 2
    freqs = ROPE_BASE ** (-jnp.arange(half, dtype=jnp.float32) / half)
    angles = positions[:, None] * freqs[None, :]
    cosine = jnp.cos(angles)[:, None, :]
    sine = jnp.sin(angles)[:, None, :]
    first = heads[..., :half]
    second = heads[..., half:]
    return jnp.concatenate([first * cosine - second * sine, first * sine + second * cosine], axis=-1)

def block_output(seq, gain, wqkv, wout):
    length = seq.shape[0]
    wide = seq.astype(jnp.float32)
    factor = lax.rsqrt(lax.optimization_barrier(jnp.mean(wide * wide, axis=-1, keepdims=True)) + NORM_EPS)
    normed = (wide * factor * gain).astype(jnp.bfloat16)
    mixed = jnp.dot(normed, wqkv, preferred_element_type=jnp.float32)
    qwidth = HEADS * HEAD_DIM
    kwidth = KV_HEADS * HEAD_DIM
    queries = mixed[:, :qwidth].reshape(length, HEADS, HEAD_DIM)
    keys = mixed[:, qwidth:qwidth + kwidth].reshape(length, KV_HEADS, HEAD_DIM)
    values = mixed[:, qwidth + kwidth:].reshape(length, KV_HEADS, HEAD_DIM).astype(jnp.bfloat16)
    positions = jnp.arange(length, dtype=jnp.float32)
    queries = rotary(queries, positions).astype(jnp.bfloat16)
    keys = rotary(keys, positions).astype(jnp.bfloat16)
    queries = queries.reshape(length, KV_HEADS, HEADS // KV_HEADS, HEAD_DIM)
    scores = jnp.einsum('qkgd,skd->kgqs', queries.astype(jnp.float32), keys.astype(jnp.float32)) * HEAD_DIM ** (-0.5)
    causal = positions[:, None] >= positions[None, :]
    scores = jnp.where(causal, scores, -1e+30)
    weights = jax.nn.softmax(scores, axis=-1).astype(jnp.bfloat16)
    attended = jnp.einsum('kgqs,skd->qkgd', weights.astype(jnp.float32), values.astype(jnp.float32))
    attended = attended.astype(jnp.bfloat16).reshape(length, qwidth)
    return jnp.dot(attended, wout, preferred_element_type=jnp.float32)

def sequence_grads(seq, cot, gain, wqkv, wout):

    def loss(gain_in, qkv_in, out_in):
        return jnp.sum(block_output(seq, gain_in, qkv_in, out_in) * cot.astype(jnp.float32))
    return jax.grad(loss, argnums=(0, 1, 2))(gain, wqkv, wout)

def adamw(param, grad, first, second, decay):
    wide = param.astype(jnp.float32)
    first_next = BETA_ONE * first + (1.0 - BETA_ONE) * grad
    second_next = BETA_TWO * second + (1.0 - BETA_TWO) * grad * grad
    update = first_next / (1.0 - BETA_ONE ** STEP_COUNT) / (jnp.sqrt(second_next / (1.0 - BETA_TWO ** STEP_COUNT)) + ADAM_EPS)
    return (wide - INNER_RATE * (update + decay * wide), first_next, second_next)

def nesterov(global_value, momentum, average):
    delta = global_value - average
    momentum_next = OUTER_MOMENTUM * momentum + delta
    return (global_value - OUTER_RATE * (delta + OUTER_MOMENTUM * momentum_next), momentum_next)

def reference(tokens, cotangent, norm_gain, qkv_weight, out_weight, gain_first, gain_second, qkv_first, qkv_second, out_first, out_second, gain_global, gain_momentum, qkv_global, qkv_momentum, out_global, out_momentum):
    seqs = tokens.reshape(N_ISLAND, N_FSDP, TOK_DEV, D)
    cots = cotangent.reshape(N_ISLAND, N_FSDP, TOK_DEV, D)

    def one_island(item):
        island_seqs, island_cots, gain, wqkv, wout = item

        def accumulate(carry, pair):
            g_gain, g_qkv, g_out = sequence_grads(pair[0], pair[1], gain, wqkv, wout)
            return ((carry[0] + g_gain, carry[1] + g_qkv.astype(jnp.float32), carry[2] + g_out.astype(jnp.float32)), None)
        start = (jnp.zeros(gain.shape, jnp.float32), jnp.zeros(wqkv.shape, jnp.float32), jnp.zeros(wout.shape, jnp.float32))
        sums, _ = lax.scan(accumulate, start, (island_seqs, island_cots))
        return sums
    gain_grad, qkv_grad, out_grad = lax.map(one_island, (seqs, cots, norm_gain, qkv_weight, out_weight))
    gain_step, gain_first_next, gain_second_next = adamw(norm_gain, gain_grad, gain_first, gain_second, 0.0)
    qkv_step, qkv_first_next, qkv_second_next = adamw(qkv_weight, qkv_grad, qkv_first, qkv_second, WEIGHT_DECAY)
    out_step, out_first_next, out_second_next = adamw(out_weight, out_grad, out_first, out_second, WEIGHT_DECAY)
    scale = 1.0 / N_ISLAND
    gain_global_next, gain_momentum_next = nesterov(gain_global, gain_momentum, lax.optimization_barrier(jnp.sum(norm_gain, axis=0)) * scale)
    qkv_global_next, qkv_momentum_next = nesterov(qkv_global, qkv_momentum, lax.optimization_barrier(jnp.sum(qkv_weight.astype(jnp.float32), axis=0)) * scale)
    out_global_next, out_momentum_next = nesterov(out_global, out_momentum, lax.optimization_barrier(jnp.sum(out_weight.astype(jnp.float32), axis=0)) * scale)
    gain_next = MIXING * gain_step + (1.0 - MIXING) * gain_global_next[None]
    qkv_next = (MIXING * qkv_step + (1.0 - MIXING) * qkv_global_next[None]).astype(jnp.bfloat16)
    out_next = (MIXING * out_step + (1.0 - MIXING) * out_global_next[None]).astype(jnp.bfloat16)
    return (gain_next, qkv_next, out_next, gain_first_next, gain_second_next, qkv_first_next, qkv_second_next, out_first_next, out_second_next, gain_global_next, gain_momentum_next, qkv_global_next, qkv_momentum_next, out_global_next, out_momentum_next)
```

```python
import functools

import jax
import jax.numpy as jnp
import numpy as np
from jax import lax
from jax.experimental import pallas as pl
from jax.experimental.pallas import tpu as pltpu
from jax.sharding import PartitionSpec as P

HEADS = 16
KV_HEADS = 4
HEAD_DIM = 64
GROUP = HEADS // KV_HEADS

BETA_ONE = 0.9
BETA_TWO = 0.95
ADAM_EPS = 1e-08
INNER_RATE = 0.001
WEIGHT_DECAY = 0.1
STEP_COUNT = 100.0
OUTER_RATE = 0.7
OUTER_MOMENTUM = 0.9
MIXING = 0.5
NORM_EPS = 1e-05
ROPE_BASE = 500000.0

MESH = pl.DeviceIdType.MESH
F32 = jnp.float32
BF16 = jnp.bfloat16

TOK = 512
D = 2048
QW = HEADS * HEAD_DIM
QKV = QW + 2 * KV_HEADS * HEAD_DIM
QROWS = 256
OROWS = 128
HALF = OROWS // 2
COLS = 256
CHUNKS = QKV // COLS
KCHUNK, VCHUNK = QW // COLS, QW // COLS + 1
QB = 256
NT = (((1,), (1,)), ((), ()))


def rope_tables():
    half = HEAD_DIM // 2
    freqs = ROPE_BASE ** (-np.arange(half, dtype=np.float64) / half)
    angles = freqs[:, None] * np.arange(TOK, dtype=np.float64)[None, :]
    return np.cos(angles).astype(np.float32), np.sin(angles).astype(np.float32)


def adamw(param, grad, first, second, decay):
    wide = param.astype(F32)
    first_next = BETA_ONE * first + (1.0 - BETA_ONE) * grad
    second_next = BETA_TWO * second + (1.0 - BETA_TWO) * grad * grad
    update = (
        first_next
        / (1.0 - BETA_ONE**STEP_COUNT)
        / (jnp.sqrt(second_next / (1.0 - BETA_TWO**STEP_COUNT)) + ADAM_EPS)
    )
    return (wide - INNER_RATE * (update + decay * wide), first_next, second_next)


def nesterov(global_value, momentum, average):
    delta = global_value - average
    momentum_next = OUTER_MOMENTUM * momentum + delta
    return (global_value - OUTER_RATE * (delta + OUTER_MOMENTUM * momentum_next), momentum_next)


def rows_of(index, size):
    return pl.ds(pl.multiple_of(index * size, size), size)


def grads_kernel(
    islands,
    x_ref, cot_ref, gain_ref, wq_ref, wo_ref, cos_ref, sin_ref, qglob_ref, qmom_ref, oglob_ref, omom_ref,
    sumq_ref, sumo_ref, sumg_ref, totq_ref, toto_ref, totg_ref, wholeq_ref, wholeo_ref,
    wq, wo, nrm, nrm_t, fac, qkv_t, k_tok, v_tok, datt_t, att_t, dm_t, dm, dk_acc, dv_acc,
    gq, go, rq, ro, ro_z, g_rows, g_recv,
    i_send, i_recv, io_recv, ig_recv, i_back, io_back, i_new, io_new,
    own_sem, agq_s, agq_r, ago_s, ago_r, rsq_s, rsq_r, rso_s, rso_r, gg_s, gg_r, is_s, is_r, ib_s, ib_r,
):
    f = lax.axis_index("fsdp")
    me = lax.axis_index("island")
    a, b = f // 2, f % 2
    qshare = QKV // islands
    oshare = D // islands

    def at_x(step):
        return lax.rem(a + step, 4)

    right = {"fsdp": at_x(1) * 2 + b}
    left = {"fsdp": at_x(3) * 2 + b}
    across = {"fsdp": a * 2 + 1 - b}
    sent = []

    def send(src, dst, s_sem, r_sem, to):
        copy = pltpu.make_async_remote_copy(
            src_ref=src, dst_ref=dst, send_sem=s_sem, recv_sem=r_sem, device_id=to, device_id_type=MESH
        )
        copy.start()
        sent.append((src, s_sem))

    def got(dst, r_sem):
        pltpu.make_async_remote_copy(
            src_ref=dst, dst_ref=dst, send_sem=r_sem, recv_sem=r_sem, device_id=across, device_id_type=MESH
        ).wait_recv()

    def left_here(src, s_sem):
        pltpu.make_async_remote_copy(
            src_ref=src, dst_ref=src, send_sem=s_sem, recv_sem=s_sem, device_id=across, device_id_type=MESH
        ).wait_send()

    barrier = pltpu.get_barrier_semaphore()

    @pl.loop(1, 8)
    def _(step):
        pl.semaphore_signal(barrier, inc=1, device_id={"fsdp": lax.rem(f + step, 8)}, device_id_type=MESH)

    @pl.loop(1, islands)
    def _(step):
        pl.semaphore_signal(
            barrier, inc=1, device_id={"island": lax.rem(me + step, islands)}, device_id_type=MESH
        )

    for i in range(islands):
        i_send[i] = wq_ref[:, i * qshare : (i + 1) * qshare]
    pl.semaphore_wait(barrier, 7 + islands - 1)

    def wq_block(x_at, z_at, c):
        return wq.at[rows_of(x_at * 2 + z_at, QROWS), pl.ds(c * COLS, COLS)]

    def own_chunk(c):
        src = wq_ref.at[:, pl.ds(c * COLS, COLS)]
        dst = wq_block(a, b, c)
        send(src, dst, agq_s.at[c, 0], agq_r.at[c, 0], across)
        send(src, dst, agq_s.at[c, 1], agq_r.at[c, 1 + b], right)
        send(src, dst, agq_s.at[c, 2], agq_r.at[c, 3 + b], left)

    def pair_chunk(c):
        block = wq_block(a, 1 - b, c)
        got(block, agq_r.at[c, 0])
        send(block, block, agq_s.at[c, 3], agq_r.at[c, 1 + 1 - b], right)
        send(block, block, agq_s.at[c, 4], agq_r.at[c, 3 + 1 - b], left)

    def pass_chunk(c):
        block = wq_block(at_x(3), 1, c)
        got(block, agq_r.at[c, 2])
        send(block, block, agq_s.at[c, 5], agq_r.at[c, 5], right)
        block = wq_block(at_x(1), 0, c)
        got(block, agq_r.at[c, 3])
        send(block, block, agq_s.at[c, 6], agq_r.at[c, 6], left)

    def have_chunk(c):
        got(wq_block(at_x(3), 0, c), agq_r.at[c, 1])
        got(wq_block(at_x(1), 1, c), agq_r.at[c, 4])
        got(wq_block(at_x(2), 1, c), agq_r.at[c, 5])
        got(wq_block(at_x(2), 0, c), agq_r.at[c, 6])

    def wo_rows(x_at, z_at, half=None):
        start = (x_at * 2 + z_at) * OROWS
        if half is None:
            return wo.at[pl.ds(pl.multiple_of(start, OROWS), OROWS)]
        return wo.at[pl.ds(pl.multiple_of(start + half * HALF, HALF), HALF)]

    def own_out():
        dst = wo_rows(a, b)
        send(wo_ref, dst, ago_s.at[0], ago_r.at[0], right)
        send(wo_ref, dst, ago_s.at[1], ago_r.at[1], left)
        send(wo_ref, dst, ago_s.at[2], ago_r.at[2], across)

    def pass_out():
        block, part = wo_rows(at_x(3), b), wo_rows(at_x(3), b, 0)
        got(block, ago_r.at[0])
        send(part, part, ago_s.at[3], ago_r.at[3], right)
        send(block, block, ago_s.at[5], ago_r.at[5], across)
        block, part = wo_rows(at_x(1), b), wo_rows(at_x(1), b, 1)
        got(block, ago_r.at[1])
        send(part, part, ago_s.at[4], ago_r.at[4], left)
        send(block, block, ago_s.at[6], ago_r.at[6], across)

    def pass_out_far():
        for half in range(2):
            part = wo_rows(at_x(2), b, half)
            got(part, ago_r.at[3 + half])
            send(part, part, ago_s.at[7 + half], ago_r.at[7 + half], across)

    def have_out():
        got(wo_rows(a, 1 - b), ago_r.at[2])
        got(wo_rows(at_x(3), 1 - b), ago_r.at[5])
        got(wo_rows(at_x(1), 1 - b), ago_r.at[6])
        for half in range(2):
            got(wo_rows(at_x(2), 1 - b, half), ago_r.at[7 + half])

    def island_send():
        @pl.loop(1, islands)
        def _(step):
            to = lax.rem(me + step, islands)
            peer = {"island": to}
            for n, (src, dst) in enumerate((
                (i_send.at[to], i_recv.at[me]),
                (wo_ref.at[:, rows_of(to, oshare)], io_recv.at[me]),
                (g_rows.at[0], ig_recv.at[me]),
            )):
                pltpu.make_async_remote_copy(
                    src_ref=src, dst_ref=dst, send_sem=is_s.at[n, step], recv_sem=is_r.at[n, step],
                    device_id=peer, device_id_type=MESH,
                ).start()
        i_recv[me] = i_send[me]
        io_recv[me] = wo_ref[:, rows_of(me, oshare)]
        ig_recv[me] = g_rows[0]

    def island_sum():
        @pl.loop(1, islands)
        def _(step):
            source = lax.rem(me - step + islands, islands)
            got(i_recv.at[source], is_r.at[0, step])
            got(io_recv.at[source], is_r.at[1, step])
            got(ig_recv.at[source], is_r.at[2, step])
        totq_ref[...] = i_recv[0].astype(F32)
        toto_ref[...] = io_recv[0].astype(F32)
        total = ig_recv[0]
        for i in range(1, islands):
            total = total + ig_recv[i]
        for i in range(8):
            totg_ref[:, i * 256 : (i + 1) * 256] = total[i : i + 1, :]

        @pl.loop(1, islands)
        def _(i):
            totq_ref[...] += i_recv[i].astype(F32)
            toto_ref[...] += io_recv[i].astype(F32)

        i_new[...] = nesterov(qglob_ref[...], qmom_ref[...], totq_ref[...] * (1.0 / islands))[0].astype(BF16)
        io_new[...] = nesterov(oglob_ref[...], omom_ref[...], toto_ref[...] * (1.0 / islands))[0].astype(BF16)

        @pl.loop(1, islands)
        def _(step):
            peer = {"island": lax.rem(me + step, islands)}
            for n, (src, dst) in enumerate(((i_new, i_back.at[me]), (io_new, io_back.at[me]))):
                pltpu.make_async_remote_copy(
                    src_ref=src, dst_ref=dst, send_sem=ib_s.at[n, step], recv_sem=ib_r.at[n, step],
                    device_id=peer, device_id_type=MESH,
                ).start()
        i_back[me] = i_new[...]
        io_back[me] = io_new[...]

    def island_whole():
        @pl.loop(1, islands)
        def _(step):
            source = lax.rem(me - step + islands, islands)
            got(i_back.at[source], ib_r.at[0, step])
            got(io_back.at[source], ib_r.at[1, step])
        for i in range(islands):
            wholeq_ref[:, i * qshare : (i + 1) * qshare] = i_back[i]
            wholeo_ref[:, i * oshare : (i + 1) * oshare] = io_back[i]

        @pl.loop(1, islands)
        def _(step):
            to = lax.rem(me + step, islands)
            left_here(i_send.at[to], is_s.at[0, step])
            left_here(wo_ref.at[:, rows_of(to, oshare)], is_s.at[1, step])
            left_here(g_rows.at[0], is_s.at[2, step])
            left_here(i_new, ib_s.at[0, step])
            left_here(io_new, ib_s.at[1, step])

    def normalise():
        @pl.loop(0, TOK // 128)
        def _(t):
            rows = rows_of(t, 128)
            wide = x_ref[rows, :].astype(F32)
            factor = lax.rsqrt(jnp.mean(wide * wide, axis=-1, keepdims=True) + NORM_EPS)
            fac[rows, :] = factor
            normed = (wide * factor * gain_ref[...]).astype(BF16)
            nrm[rows, :] = normed
            nrm_t[:, rows] = normed.astype(F32).T.astype(BF16)

    def turn(first, second, sign):
        cosine, sine = cos_ref[...], sin_ref[...] * sign
        return first * cosine - second * sine, first * sine + second * cosine

    def project(c):
        mixed = jnp.dot(nrm[...], wq[:, c * COLS : (c + 1) * COLS], preferred_element_type=F32)
        if c == VCHUNK:
            mixed = mixed.astype(BF16).astype(F32)
        mixed_t = mixed.T
        for n in range(COLS // HEAD_DIM):
            at = n * HEAD_DIM
            head = mixed_t[at : at + HEAD_DIM, :]
            if c != VCHUNK:
                first, second = turn(head[: HEAD_DIM // 2], head[HEAD_DIM // 2 :], 1.0)
                head = jnp.concatenate([first, second], axis=0)
            held = head.astype(BF16)
            if c < KCHUNK:
                held = (held.astype(F32) * HEAD_DIM ** (-0.5)).astype(BF16)
            qkv_t[c * COLS + at : c * COLS + at + HEAD_DIM, :] = held
            if c == KCHUNK:
                k_tok[n] = held.astype(F32).T.astype(BF16)
            if c == VCHUNK:
                v_tok[n] = held.astype(F32).T.astype(BF16)

    def project_back():
        @pl.loop(0, 8)
        def _(j):
            rows = rows_of(j, OROWS)
            datt_t[rows, :] = lax.dot_general(
                wo[rows, :], cot_ref[...], NT, preferred_element_type=F32
            ).astype(BF16)

    def attend(g):
        krows = slice(QW + g * HEAD_DIM, QW + (g + 1) * HEAD_DIM)
        vrows = slice(QW + (KV_HEADS + g) * HEAD_DIM, QW + (KV_HEADS + g + 1) * HEAD_DIM)
        dk_acc[...] = jnp.zeros_like(dk_acc)
        dv_acc[...] = jnp.zeros_like(dv_acc)

        @pl.loop(0, GROUP)
        def _(n):
            rows = rows_of(g * GROUP + n, HEAD_DIM)
            for q_at in range(0, TOK, QB):
                keys = q_at + QB
                queries = qkv_t[rows, q_at : q_at + QB]
                scores = jnp.dot(k_tok[g, :keys, :], queries, preferred_element_type=F32)
                key_at = lax.broadcasted_iota(jnp.int32, (keys, QB), 0)
                query_at = lax.broadcasted_iota(jnp.int32, (keys, QB), 1) + q_at
                scores = jnp.where(query_at >= key_at, scores, -1e30)
                top = jnp.max(scores, axis=0, keepdims=True)
                raised = jnp.exp(scores - top)
                soft = raised * (1.0 / jnp.sum(raised, axis=0, keepdims=True))
                weights = soft.astype(BF16)
                out = jnp.dot(qkv_t[vrows, :keys], weights, preferred_element_type=F32)
                att_t[rows, q_at : q_at + QB] = out.astype(BF16)
                dout = datt_t[rows, q_at : q_at + QB]
                dweights = jnp.dot(v_tok[g, :keys, :], dout, preferred_element_type=F32)
                dot_out = jnp.sum(out * dout.astype(F32), axis=0, keepdims=True)
                dscores = (soft * (dweights - dot_out)).astype(BF16)
                dqueries = jnp.dot(qkv_t[krows, :keys], dscores, preferred_element_type=F32)
                dqueries = (dqueries * HEAD_DIM ** (-0.5)).astype(BF16).astype(F32)
                half = HEAD_DIM // 2
                cosine, sine = cos_ref[:, q_at : q_at + QB], sin_ref[:, q_at : q_at + QB]
                first, second = dqueries[:half], dqueries[half:]
                dm_t[rows, q_at : q_at + QB] = jnp.concatenate(
                    [first * cosine + second * sine, second * cosine - first * sine], axis=0
                ).astype(BF16)
                dk_acc[:, :keys] += lax.dot_general(queries, dscores, NT, preferred_element_type=F32)
                dv_acc[:, :keys] += lax.dot_general(dout, weights, NT, preferred_element_type=F32)

        dkeys = dk_acc[...].astype(BF16).astype(F32)
        first, second = turn(dkeys[: HEAD_DIM // 2], dkeys[HEAD_DIM // 2 :], -1.0)
        dm_t[krows, :] = jnp.concatenate([first, second], axis=0).astype(BF16)
        dm_t[vrows, :] = dv_acc[...].astype(BF16)

    def gq_block(x_at, z_at, c):
        return gq.at[rows_of(x_at * 2 + z_at, QROWS), pl.ds(c * COLS, COLS)]

    def rq_at(n, c):
        return rq.at[n, :, pl.ds(c * COLS, COLS)]

    def grad_chunk(c):
        cols = slice(c * COLS, (c + 1) * COLS)

        @pl.loop(0, 8)
        def _(j):
            rows = rows_of(j, QROWS)
            gq[rows, cols] = lax.dot_general(
                nrm_t[rows, :], dm_t[cols, :], NT, preferred_element_type=F32
            ).astype(BF16)

        for n, (block, to) in enumerate((
            (gq_block(at_x(2), 0, c), left),
            (gq_block(at_x(2), 1, c), right),
            (gq_block(at_x(3), 1, c), left),
            (gq_block(at_x(1), 0, c), right),
        )):
            send(block, rq_at(n, c), rsq_s.at[c, n], rsq_r.at[c, n], to)
        dm[:, cols] = dm_t[cols, :].astype(F32).T.astype(BF16)

    def add_chunk(c):
        for n, (block, to) in enumerate(((gq_block(at_x(3), 0, c), left), (gq_block(at_x(1), 1, c), right))):
            got(rq_at(n, c), rsq_r.at[c, n])
            block[...] = (block[...].astype(F32) + rq_at(n, c)[...].astype(F32)).astype(BF16)
            send(block, rq_at(4 + n, c), rsq_s.at[c, 4 + n], rsq_r.at[c, 4 + n], to)

    def fold_chunk(c):
        for n in range(2, 6):
            got(rq_at(n, c), rsq_r.at[c, n])

        def whole(z_at, first, second):
            return (
                gq_block(a, z_at, c)[...].astype(F32)
                + rq.at[first, :, pl.ds(c * COLS, COLS)][...].astype(F32)
                + rq.at[second, :, pl.ds(c * COLS, COLS)][...].astype(F32)
            )

        block = gq_block(a, 1 - b, c)
        block[...] = whole(1 - b, 2 + b, 5 - b).astype(BF16)
        send(block, rq_at(6, c), rsq_s.at[c, 6], rsq_r.at[c, 6], across)
        sumq_ref[:, c * COLS : (c + 1) * COLS] = whole(b, 3 - b, 4 + b)

    def end_chunk(c):
        got(rq_at(6, c), rsq_r.at[c, 6])
        sumq_ref[:, c * COLS : (c + 1) * COLS] += rq_at(6, c)[...].astype(F32)

    def go_rows(x_at, z_at, half=None):
        start = (x_at * 2 + z_at) * OROWS
        if half is None:
            return go.at[pl.ds(pl.multiple_of(start, OROWS), OROWS)]
        return go.at[pl.ds(pl.multiple_of(start + half * HALF, HALF), HALF)]

    def grad_out(g):
        @pl.loop(0, 2)
        def _(z_at):
            rows = rows_of(2 * g + z_at, OROWS)
            go[rows, :] = jnp.dot(att_t[rows, :], cot_ref[...], preferred_element_type=F32).astype(BF16)

        send(go_rows(g, 1 - b), ro_z.at[g], rso_s.at[6 + g], rso_r.at[6 + g], across)

    def pair_out(step):
        x_at = at_x(step)
        got(ro_z.at[x_at], rso_r.at[6 + x_at])
        block = go_rows(x_at, b)
        block[...] = (block[...].astype(F32) + ro_z[x_at].astype(F32)).astype(BF16)

    def ring_out():
        pair_out(2)
        send(go_rows(at_x(2), b, 0), ro.at[0], rso_s.at[0], rso_r.at[0], left)
        send(go_rows(at_x(2), b, 1), ro.at[1], rso_s.at[1], rso_r.at[1], right)
        pair_out(3)
        send(go_rows(at_x(3), b, 1), ro.at[2], rso_s.at[2], rso_r.at[2], left)
        pair_out(1)
        send(go_rows(at_x(1), b, 0), ro.at[3], rso_s.at[3], rso_r.at[3], right)
        pair_out(0)

    def add_out():
        for n, (block, to) in enumerate(((go_rows(at_x(3), b, 0), left), (go_rows(at_x(1), b, 1), right))):
            got(ro.at[n], rso_r.at[n])
            block[...] = (block[...].astype(F32) + ro[n].astype(F32)).astype(BF16)
            send(block, ro.at[4 + n], rso_s.at[4 + n], rso_r.at[4 + n], to)

    def end_out():
        for n in range(2, 6):
            got(ro.at[n], rso_r.at[n])
        sumo_ref[:HALF, :] = go_rows(a, b, 0)[...].astype(F32) + ro[3].astype(F32) + ro[4].astype(F32)
        sumo_ref[HALF:, :] = go_rows(a, b, 1)[...].astype(F32) + ro[2].astype(F32) + ro[5].astype(F32)

    def gain_grad():
        @pl.loop(0, 8)
        def _(j):
            dnormed = lax.dot_general(
                dm[...], wq[rows_of(j, QROWS), :], NT, preferred_element_type=F32
            ).astype(BF16).astype(F32)
            wide = x_ref[:, rows_of(j, QROWS)].astype(F32) * fac[...]
            g_rows[1, pl.ds(j, 1), :] = jnp.sum(dnormed * wide, axis=0, keepdims=True)

        @pl.loop(1, 8)
        def _(step):
            pltpu.make_async_remote_copy(
                src_ref=g_rows.at[1], dst_ref=g_recv.at[f], send_sem=gg_s.at[step], recv_sem=gg_r.at[step],
                device_id={"fsdp": lax.rem(f + step, 8)}, device_id_type=MESH,
            ).start()
        g_recv[f] = g_rows[1]

    def gain_sum():
        @pl.loop(1, 8)
        def _(step):
            got(g_recv.at[lax.rem(f - step + 8, 8)], gg_r.at[step])
        total = g_recv[0]
        for i in range(1, 8):
            total = total + g_recv[i]
        for i in range(8):
            sumg_ref[:, i * 256 : (i + 1) * 256] = total[i : i + 1, :]

        @pl.loop(1, 8)
        def _(step):
            left_here(g_rows.at[1], gg_s.at[step])

    for i in range(8):
        g_rows[0, i : i + 1, :] = gain_ref[:, i * 256 : (i + 1) * 256]
    keep = [
        pltpu.make_async_copy(wq_ref, wq.at[rows_of(f, QROWS)], own_sem.at[0]),
        pltpu.make_async_copy(wo_ref, wo.at[rows_of(f, OROWS)], own_sem.at[1]),
    ]
    order = [KCHUNK, VCHUNK, 0, 1, 2, 3]
    own_chunk(order[0])
    own_out()
    own_chunk(order[1])
    for copy in keep:
        copy.start()
    island_send()
    normalise()
    for copy in keep:
        copy.wait()
    pair_chunk(order[0])
    pass_out()
    own_chunk(order[2])
    pair_chunk(order[1])
    pass_chunk(order[0])
    pass_out_far()
    own_chunk(order[3])
    pair_chunk(order[2])
    pass_chunk(order[1])
    have_chunk(order[0])
    project(order[0])
    own_chunk(order[4])
    pair_chunk(order[3])
    pass_chunk(order[2])
    have_chunk(order[1])
    project(order[1])
    island_sum()
    own_chunk(order[5])
    pair_chunk(order[4])
    pass_chunk(order[3])
    have_out()
    project_back()
    have_chunk(order[2])
    project(order[2])
    pair_chunk(order[5])
    pass_chunk(order[4])
    attend(0)
    grad_chunk(0)
    grad_out(0)
    pass_chunk(order[5])
    have_chunk(order[3])
    project(order[3])
    add_chunk(0)
    attend(1)
    grad_chunk(1)
    grad_out(1)
    have_chunk(order[4])
    project(order[4])
    add_chunk(1)
    fold_chunk(0)
    attend(2)
    grad_chunk(2)
    grad_out(2)
    have_chunk(order[5])
    project(order[5])
    add_chunk(2)
    fold_chunk(1)
    attend(3)
    grad_out(3)
    grad_chunk(3)
    grad_chunk(KCHUNK)
    grad_chunk(VCHUNK)
    add_chunk(3)
    fold_chunk(2)
    ring_out()
    add_chunk(KCHUNK)
    fold_chunk(3)
    add_chunk(VCHUNK)
    add_out()
    gain_grad()
    end_chunk(0)
    end_chunk(1)
    fold_chunk(KCHUNK)
    island_whole()
    fold_chunk(VCHUNK)
    end_chunk(2)
    end_chunk(3)
    end_out()
    end_chunk(KCHUNK)
    gain_sum()
    end_chunk(VCHUNK)
    for src, s_sem in sent:
        left_here(src, s_sem)


def grads(islands, x, cot, gain, wq, wo, qglob, qmom, oglob, omom):
    qshare, oshare = QKV // islands, D // islands
    cosine, sine = rope_tables()
    vmem = pl.BlockSpec(memory_space=pltpu.VMEM)
    dma = pltpu.SemaphoreType.DMA
    return pl.pallas_call(
        functools.partial(grads_kernel, islands),
        out_shape=[
            jax.ShapeDtypeStruct((QROWS, QKV), F32),
            jax.ShapeDtypeStruct((OROWS, D), F32),
            jax.ShapeDtypeStruct((1, D), F32),
            jax.ShapeDtypeStruct((QROWS, qshare), F32),
            jax.ShapeDtypeStruct((OROWS, oshare), F32),
            jax.ShapeDtypeStruct((1, D), F32),
            jax.ShapeDtypeStruct((QROWS, QKV), BF16),
            jax.ShapeDtypeStruct((OROWS, D), BF16),
        ],
        in_specs=[vmem] * 11,
        out_specs=[vmem] * 8,
        scratch_shapes=[
            pltpu.VMEM((D, QKV), BF16),
            pltpu.VMEM((QW, D), BF16),
            pltpu.VMEM((TOK, D), BF16),
            pltpu.VMEM((D, TOK), BF16),
            pltpu.VMEM((TOK, 1), F32),
            pltpu.VMEM((QKV, TOK), BF16),
            pltpu.VMEM((KV_HEADS, TOK, HEAD_DIM), BF16),
            pltpu.VMEM((KV_HEADS, TOK, HEAD_DIM), BF16),
            pltpu.VMEM((QW, TOK), BF16),
            pltpu.VMEM((QW, TOK), BF16),
            pltpu.VMEM((QKV, TOK), BF16),
            pltpu.VMEM((TOK, QKV), BF16),
            pltpu.VMEM((HEAD_DIM, TOK), F32),
            pltpu.VMEM((HEAD_DIM, TOK), F32),
            pltpu.VMEM((D, QKV), BF16),
            pltpu.VMEM((QW, D), BF16),
            pltpu.VMEM((7, QROWS, QKV), BF16),
            pltpu.VMEM((6, HALF, D), BF16),
            pltpu.VMEM((4, OROWS, D), BF16),
            pltpu.VMEM((2, 8, 256), F32),
            pltpu.VMEM((8, 8, 256), F32),
            pltpu.VMEM((islands, QROWS, qshare), BF16),
            pltpu.VMEM((islands, QROWS, qshare), BF16),
            pltpu.VMEM((islands, OROWS, oshare), BF16),
            pltpu.VMEM((islands, 8, 256), F32),
            pltpu.VMEM((islands, QROWS, qshare), BF16),
            pltpu.VMEM((islands, OROWS, oshare), BF16),
            pltpu.VMEM((QROWS, qshare), BF16),
            pltpu.VMEM((OROWS, oshare), BF16),
            dma((2,)),
            dma((CHUNKS, 7)), dma((CHUNKS, 7)),
            dma((9,)), dma((9,)),
            dma((CHUNKS, 7)), dma((CHUNKS, 7)),
            dma((10,)), dma((10,)),
            dma((8,)), dma((8,)),
            dma((3, islands)), dma((3, islands)),
            dma((2, islands)), dma((2, islands)),
        ],
        compiler_params=pltpu.CompilerParams(
            collective_id=0, has_side_effects=True, vmem_limit_bytes=63 * 2**20
        ),
        name="grads",
    )(x, cot, gain, wq, wo, jnp.asarray(cosine), jnp.asarray(sine), qglob, qmom, oglob, omom)


def update_kernel(
    islands,
    gain_ref, wq_ref, wo_ref, gf_ref, gs_ref, qf_ref, qs_ref, of_ref, os_ref,
    gg_ref, gm_ref, qg_ref, qm_ref, og_ref, om_ref,
    sumq_ref, sumo_ref, sumg_ref, totq_ref, toto_ref, totg_ref, wholeq_ref, wholeo_ref,
    gain_o, wq_o, wo_o, gf_o, gs_o, qf_o, qs_o, of_o, os_o, gg_o, gm_o, qg_o, qm_o, og_o, om_o,
):
    scale = 1.0 / islands
    for w, s, m1, m2, whole, w_o, m1_o, m2_o in (
        (wq_ref, sumq_ref, qf_ref, qs_ref, wholeq_ref, wq_o, qf_o, qs_o),
        (wo_ref, sumo_ref, of_ref, os_ref, wholeo_ref, wo_o, of_o, os_o),
    ):
        stepped, first, second = adamw(w[...], s[...], m1[...], m2[...], WEIGHT_DECAY)
        w_o[...] = (MIXING * stepped + (1.0 - MIXING) * whole[...].astype(F32)).astype(BF16)
        m1_o[...] = first
        m2_o[...] = second

    @pl.when(pl.program_id(0) == 0)
    def _():
        stepped, first, second = adamw(gain_ref[...], sumg_ref[...], gf_ref[...], gs_ref[...], 0.0)
        outer, momentum = nesterov(gg_ref[...], gm_ref[...], totg_ref[...] * scale)
        gain_o[...] = MIXING * stepped + (1.0 - MIXING) * outer
        gf_o[...] = first
        gs_o[...] = second
        gg_o[...] = outer
        gm_o[...] = momentum
        qg_o[...], qm_o[...] = nesterov(qg_ref[...], qm_ref[...], totq_ref[...] * scale)
        og_o[...], om_o[...] = nesterov(og_ref[...], om_ref[...], toto_ref[...] * scale)


def update(islands, state, sums):
    steps = 4

    def spec(array):
        rows, cols = array.shape
        if cols in (QKV, D) and rows > 1:
            return pl.BlockSpec((rows // steps, cols), lambda i: (i, 0))
        return pl.BlockSpec((rows, cols), lambda i: (0, 0))

    outs = [state[n] for n in (0, 1, 2, 3, 4, 5, 6, 7, 8, 9, 10, 11, 12, 13, 14)]
    return pl.pallas_call(
        functools.partial(update_kernel, islands),
        grid=(steps,),
        out_shape=[jax.ShapeDtypeStruct(o.shape, o.dtype) for o in outs],
        in_specs=[spec(v) for v in (*state, *sums)],
        out_specs=[spec(o) for o in outs],
        compiler_params=pltpu.CompilerParams(vmem_limit_bytes=32 * 2**20),
        name="update",
    )(*state, *sums)


def shards(
    tokens, cotangent, norm_gain, qkv_weight, out_weight, gain_first, gain_second,
    qkv_first, qkv_second, out_first, out_second,
    gain_global, gain_momentum, qkv_global, qkv_momentum, out_global, out_momentum,
):
    islands = lax.axis_size("island")
    wq, wo = qkv_weight[0], out_weight[0]
    sums = grads(
        islands, tokens, cotangent, norm_gain, wq, wo, qkv_global, qkv_momentum, out_global, out_momentum
    )
    state = (
        norm_gain, wq, wo, gain_first, gain_second, qkv_first[0], qkv_second[0], out_first[0], out_second[0],
        gain_global[None], gain_momentum[None], qkv_global, qkv_momentum, out_global, out_momentum,
    )
    (
        gain_next, wq_next, wo_next, gf, gs, qf, qs, of, os_, gg, gm, qg, qm, og, om
    ) = update(islands, state, sums)
    return (
        gain_next, wq_next[None], wo_next[None], gf, gs, qf[None], qs[None], of[None], os_[None],
        gg[0], gm[0], qg, qm, og, om,
    )


def solution(mesh):
    placed = (
        P(("island", "fsdp"), None),
        P(("island", "fsdp"), None),
        P("island", None),
        P("island", "fsdp", None),
        P("island", "fsdp", None),
        P("island", None),
        P("island", None),
        P("island", "fsdp", None),
        P("island", "fsdp", None),
        P("island", "fsdp", None),
        P("island", "fsdp", None),
        P(),
        P(),
        P("fsdp", "island"),
        P("fsdp", "island"),
        P("fsdp", "island"),
        P("fsdp", "island"),
    )
    return jax.shard_map(
        shards,
        mesh=mesh,
        in_specs=placed,
        out_specs=(
            P("island", None),
            P("island", "fsdp", None),
            P("island", "fsdp", None),
            P("island", None),
            P("island", None),
            P("island", "fsdp", None),
            P("island", "fsdp", None),
            P("island", "fsdp", None),
            P("island", "fsdp", None),
            P(),
            P(),
            P("fsdp", "island"),
            P("fsdp", "island"),
            P("fsdp", "island"),
            P("fsdp", "island"),
        ),
        check_vma=False,
    )
```

```python
import functools

import jax
import jax.numpy as jnp
import numpy as np
from jax import lax
from jax.experimental import pallas as pl
from jax.experimental.pallas import tpu as pltpu
from jax.sharding import PartitionSpec as P

HEADS = 16
KV_HEADS = 4
HEAD_DIM = 64
GROUP = HEADS // KV_HEADS

BETA_ONE = 0.9
BETA_TWO = 0.95
ADAM_EPS = 1e-08
INNER_RATE = 0.001
WEIGHT_DECAY = 0.1
STEP_COUNT = 100.0
OUTER_RATE = 0.7
OUTER_MOMENTUM = 0.9
MIXING = 0.5
NORM_EPS = 1e-05
ROPE_BASE = 500000.0

MESH = pl.DeviceIdType.MESH
F32 = jnp.float32
BF16 = jnp.bfloat16

TOK = 512
D = 2048
QW = HEADS * HEAD_DIM
QKV = QW + 2 * KV_HEADS * HEAD_DIM
QROWS = 256
OROWS = 128
HALF = OROWS // 2
OPAIRED = 512
COLS = 256
CHUNKS = QKV // COLS
KCHUNK, VCHUNK = QW // COLS, QW // COLS + 1
QB = 256
NT = (((1,), (1,)), ((), ()))


def rope_tables():
    half = HEAD_DIM // 2
    freqs = ROPE_BASE ** (-np.arange(half, dtype=np.float64) / half)
    angles = freqs[:, None] * np.arange(TOK, dtype=np.float64)[None, :]
    return np.cos(angles).astype(np.float32), np.sin(angles).astype(np.float32)


def adamw(param, grad, first, second, decay):
    wide = param.astype(F32)
    first_next = BETA_ONE * first + (1.0 - BETA_ONE) * grad
    second_next = BETA_TWO * second + (1.0 - BETA_TWO) * grad * grad
    update = (
        first_next
        * (1.0 / (1.0 - BETA_ONE**STEP_COUNT))
        / (jnp.sqrt(second_next * (1.0 / (1.0 - BETA_TWO**STEP_COUNT))) + ADAM_EPS)
    )
    return (wide - INNER_RATE * (update + decay * wide), first_next, second_next)


def nesterov(global_value, momentum, average):
    delta = global_value - average
    momentum_next = OUTER_MOMENTUM * momentum + delta
    return (global_value - OUTER_RATE * (delta + OUTER_MOMENTUM * momentum_next), momentum_next)


def rows_of(index, size):
    return pl.ds(pl.multiple_of(index * size, size), size)


def grads_kernel(
    islands,
    x_in, cot_in, gain_in, wq_in, wo_in, cos_in, sin_in, qglob_in, qmom_in, oglob_in, omom_in,
    sumq_out, sumo_out, sumg_out, totq_out, toto_out, totg_out, wholeq_out, wholeo_out,
    x_ref, cot_ref, gain_ref, cos_ref, sin_ref, qglob_ref, qmom_ref, oglob_ref, omom_ref,
    sumq_ref, sumo_ref, sumg_ref, totq_ref, toto_ref, totg_ref, wholeq_ref, wholeo_ref,
    wq, wo, nrm, nrm_t, fac, qkv_t, k_tok, v_tok, datt_t, att_t, dm_t, dm, dk_acc, dv_acc,
    gq, go, rq, ro, ro_z, g_rows, g_recv,
    i_own, io_own, i_core, io_core, ig_core, i_ring, io_ring, ig_ring, i_far, io_far, ig_far, ig_own, i_back, io_back,
    own_sem, out_sem, agq_s, agq_r, ago_s, ago_r, rsq_s, rsq_r, rso_s, rso_r, gg_s, gg_r, is_s, is_r,
):
    f = lax.axis_index("fsdp")
    me = lax.axis_index("island")
    a, b = f // 2, f % 2
    y, zh, core = me // 4, (me // 2) % 2, me % 2
    qshare = QKV // islands
    oshare = D // islands

    def at_x(step):
        return lax.rem(a + step, 4)

    right = {"fsdp": at_x(1) * 2 + b}
    left = {"fsdp": at_x(3) * 2 + b}
    across = {"fsdp": a * 2 + 1 - b}
    sent = []

    def send(src, dst, s_sem, r_sem, to):
        copy = pltpu.make_async_remote_copy(
            src_ref=src, dst_ref=dst, send_sem=s_sem, recv_sem=r_sem, device_id=to, device_id_type=MESH
        )
        copy.start()
        sent.append((src, s_sem))

    def got(dst, r_sem):
        pltpu.make_async_remote_copy(
            src_ref=dst, dst_ref=dst, send_sem=r_sem, recv_sem=r_sem, device_id=across, device_id_type=MESH
        ).wait_recv()

    def left_here(src, s_sem):
        pltpu.make_async_remote_copy(
            src_ref=src, dst_ref=src, send_sem=s_sem, recv_sem=s_sem, device_id=across, device_id_type=MESH
        ).wait_send()

    barrier = pltpu.get_barrier_semaphore()

    @pl.loop(1, 8)
    def _(step):
        pl.semaphore_signal(barrier, inc=1, device_id={"fsdp": lax.rem(f + step, 8)}, device_id_type=MESH)

    other_core = {"island": me + 1 - 2 * core}
    other_far = {"island": me + 2 - 4 * zh}

    def other_y(step):
        return lax.rem(y + step, 4)

    def on_y(step):
        return {"island": other_y(step) * 4 + zh * 2 + core}

    pl.semaphore_signal(barrier, inc=1, device_id=other_core, device_id_type=MESH)
    pl.semaphore_signal(barrier, inc=1, device_id=other_far, device_id_type=MESH)
    for step in range(1, 4):
        pl.semaphore_signal(barrier, inc=1, device_id=on_y(step), device_id_type=MESH)
    loads = [
        pltpu.make_async_copy(src, dst, own_sem.at[n])
        for n, (src, dst) in enumerate((
            (x_in, x_ref), (gain_in, gain_ref), (wq_in, wq.at[rows_of(f, QROWS)]), (wo_in, wo.at[rows_of(f, OROWS)]),
            (cos_in, cos_ref), (sin_in, sin_ref), (cot_in, cot_ref), (qglob_in, qglob_ref), (qmom_in, qmom_ref),
            (oglob_in, oglob_ref), (omom_in, omom_ref),
        ))
    ]
    for copy in loads:
        copy.start()
    stores = []

    def store(src, dst):
        copy = pltpu.make_async_copy(src, dst, out_sem.at[len(stores)])
        copy.start()
        stores.append(copy)

    pl.semaphore_wait(barrier, 7 + 5)

    def wq_block(c):
        def block(x_at, z_at, half=None):
            start, size = (x_at * 2 + z_at) * QROWS, QROWS
            if half is not None:
                start, size = start + half * (QROWS // 2), QROWS // 2
            return wq.at[pl.ds(pl.multiple_of(start, size), size), pl.ds(c * COLS, COLS)]

        return block

    def wo_block(col, cols):
        def block(x_at, z_at, half=None):
            start, size = (x_at * 2 + z_at) * OROWS, OROWS
            if half is not None:
                start, size = start + half * HALF, HALF
            return wo.at[pl.ds(pl.multiple_of(start, size), size), pl.ds(col, cols)]

        return block

    class Paired:
        def __init__(self, src, block, n):
            self.src, self.block, self.s, self.r = src, block, agq_s.at[n], agq_r.at[n]

        def own(self):
            dst = self.block(a, b)
            send(self.src, dst, self.s.at[0], self.r.at[0], across)
            send(self.src, dst, self.s.at[1], self.r.at[1 + b], right)
            send(self.src, dst, self.s.at[2], self.r.at[3 + b], left)

        def pair(self):
            block = self.block(a, 1 - b)
            got(block, self.r.at[0])
            send(block, block, self.s.at[3], self.r.at[1 + 1 - b], right)
            send(block, block, self.s.at[4], self.r.at[3 + 1 - b], left)

        def onward(self):
            block = self.block(at_x(3), 1)
            got(block, self.r.at[2])
            send(block, block, self.s.at[5], self.r.at[5], right)
            block = self.block(at_x(1), 0)
            got(block, self.r.at[3])
            send(block, block, self.s.at[6], self.r.at[6], left)

        def have(self):
            got(self.block(at_x(3), 0), self.r.at[1])
            got(self.block(at_x(1), 1), self.r.at[4])
            got(self.block(at_x(2), 1), self.r.at[5])
            got(self.block(at_x(2), 0), self.r.at[6])

    class Ringed:
        def __init__(self, src, block, n):
            self.src, self.block, self.s, self.r = src, block, ago_s.at[n], ago_r.at[n]

        def own(self):
            dst = self.block(a, b)
            send(self.src, dst, self.s.at[0], self.r.at[0], right)
            send(self.src, dst, self.s.at[1], self.r.at[1], left)
            send(self.src, dst, self.s.at[2], self.r.at[2], across)

        def onward(self):
            for n, (x_at, to) in enumerate(((at_x(3), right), (at_x(1), left))):
                block, part = self.block(x_at, b), self.block(x_at, b, n)
                got(block, self.r.at[n])
                send(part, part, self.s.at[3 + n], self.r.at[3 + n], to)
                send(block, block, self.s.at[5 + n], self.r.at[5 + n], across)

        def far(self):
            for n in range(2):
                part = self.block(at_x(2), b, n)
                got(part, self.r.at[3 + n])
                send(part, part, self.s.at[7 + n], self.r.at[7 + n], across)

        def have(self):
            got(self.block(a, 1 - b), self.r.at[2])
            got(self.block(at_x(3), 1 - b), self.r.at[5])
            got(self.block(at_x(1), 1 - b), self.r.at[6])
            for n in range(2):
                got(self.block(at_x(2), 1 - b, n), self.r.at[7 + n])

    chunks = [
        (Paired if c != 3 else Ringed)(wq_in.at[:, pl.ds(c * COLS, COLS)], wq_block(c), c if c != 3 else 1)
        for c in range(CHUNKS)
    ]
    out_paired = Paired(wo_in.at[:, pl.ds(0, OPAIRED)], wo_block(0, OPAIRED), 3)
    out_ringed = Ringed(wo_in.at[:, pl.ds(OPAIRED, D - OPAIRED)], wo_block(OPAIRED, D - OPAIRED), 0)

    def island_start():
        own = wq.at[rows_of(f, QROWS)]
        for i in range(islands):
            if i % 4 == 0:
                turned = own[:, i * qshare : (i + 4) * qshare].astype(F32).T.astype(BF16)
            i_own[i // 2, i % 2] = turned[i % 4 * qshare : (i % 4 + 1) * qshare]
            io_own[i // 2, i % 2] = wo[rows_of(f, OROWS), i * oshare : (i + 1) * oshare]
        for i in range(8):
            ig_own[i : i + 1, :] = gain_ref[:, i * 256 : (i + 1) * 256]
        send(i_own.at[:, 1 - core], i_core, is_s.at[0], is_r.at[0], other_core)
        send(io_own.at[:, 1 - core], io_core, is_s.at[1], is_r.at[1], other_core)
        send(ig_own, ig_core, is_s.at[2], is_r.at[2], other_core)

    def island_ring():
        got(i_core, is_r.at[0])
        got(io_core, is_r.at[1])
        got(ig_core, is_r.at[2])

        @pl.loop(0, 8)
        def _(n):
            i_core[n] = (i_core[n].astype(F32) + i_own[n, core].astype(F32)).astype(BF16)
            io_core[n] = (io_core[n].astype(F32) + io_own[n, core].astype(F32)).astype(BF16)

        ig_core[...] += ig_own[...]
        for step in range(1, 4):
            two = pl.ds(other_y(step) * 2, 2)
            send(i_core.at[two], i_ring.at[y], is_s.at[3 * step], is_r.at[3 * step], on_y(step))
            send(io_core.at[two], io_ring.at[y], is_s.at[3 * step + 1], is_r.at[3 * step + 1], on_y(step))
            send(ig_core, ig_ring.at[y], is_s.at[3 * step + 2], is_r.at[3 * step + 2], on_y(step))
        two = pl.ds(y * 2, 2)
        i_ring[y] = i_core[two]
        io_ring[y] = io_core[two]
        ig_ring[y] = ig_core[...]

    def island_far():
        for step in range(1, 4):
            source = other_y(4 - step)
            got(i_ring.at[source], is_r.at[3 * step])
            got(io_ring.at[source], is_r.at[3 * step + 1])
            got(ig_ring.at[source], is_r.at[3 * step + 2])
        i_ring[0] = (
            i_ring[0].astype(F32) + i_ring[1].astype(F32) + i_ring[2].astype(F32) + i_ring[3].astype(F32)
        ).astype(BF16)
        io_ring[0] = (
            io_ring[0].astype(F32) + io_ring[1].astype(F32) + io_ring[2].astype(F32) + io_ring[3].astype(F32)
        ).astype(BF16)
        ig_ring[0] = ig_ring[0] + ig_ring[1] + ig_ring[2] + ig_ring[3]
        send(i_ring.at[0, 1 - zh], i_far, is_s.at[12], is_r.at[12], other_far)
        send(io_ring.at[0, 1 - zh], io_far, is_s.at[13], is_r.at[13], other_far)
        send(ig_ring.at[0], ig_far, is_s.at[14], is_r.at[14], other_far)

    def island_sum():
        got(i_far, is_r.at[12])
        got(io_far, is_r.at[13])
        got(ig_far, is_r.at[14])
        totq_ref[...] = i_ring[0, zh].astype(F32) + i_far[...].astype(F32)
        toto_ref[...] = io_ring[0, zh].astype(F32) + io_far[...].astype(F32)
        total = ig_ring[0] + ig_far[...]
        for i in range(8):
            totg_ref[:, i * 256 : (i + 1) * 256] = total[i : i + 1, :]
        here = me // 2
        i_back[here, core] = nesterov(
            qglob_ref[...], qmom_ref[...], totq_ref[...] * (1.0 / islands)
        )[0].astype(BF16)
        io_back[here, core] = nesterov(
            oglob_ref[...], omom_ref[...], toto_ref[...] * (1.0 / islands)
        )[0].astype(BF16)
        send(i_back.at[here, core], i_back.at[here, core], is_s.at[15], is_r.at[15], other_far)
        send(io_back.at[here, core], io_back.at[here, core], is_s.at[16], is_r.at[16], other_far)
        store(totq_ref, totq_out)
        store(toto_ref, toto_out)
        store(totg_ref, totg_out)

    def back_ring():
        there = y * 2 + 1 - zh
        got(i_back.at[there, core], is_r.at[15])
        got(io_back.at[there, core], is_r.at[16])
        mine = i_back.at[pl.ds(y * 2, 2), core], io_back.at[pl.ds(y * 2, 2), core]
        for step in range(1, 4):
            for n in range(2):
                at = 17 + 2 * (step - 1) + n
                send(mine[n], mine[n], is_s.at[at], is_r.at[at], on_y(step))

    def back_core():
        for step in range(1, 4):
            source = pl.ds(other_y(4 - step) * 2, 2)
            got(i_back.at[source, core], is_r.at[17 + 2 * (step - 1)])
            got(io_back.at[source, core], is_r.at[18 + 2 * (step - 1)])
        send(i_back.at[:, core], i_back.at[:, core], is_s.at[23], is_r.at[23], other_core)
        send(io_back.at[:, core], io_back.at[:, core], is_s.at[24], is_r.at[24], other_core)

    def island_whole():
        got(i_back.at[:, 1 - core], is_r.at[23])
        got(io_back.at[:, 1 - core], is_r.at[24])
        for i in range(islands // 4):
            four = jnp.concatenate([i_back[2 * i + n // 2, n % 2] for n in range(4)], axis=0)
            wholeq_ref[:, i * 4 * qshare : (i + 1) * 4 * qshare] = four.astype(F32).T.astype(BF16)
        for i in range(islands):
            wholeo_ref[:, i * oshare : (i + 1) * oshare] = io_back[i // 2, i % 2]
        store(wholeq_ref, wholeq_out)
        store(wholeo_ref, wholeo_out)

    def normalise():
        @pl.loop(0, TOK // 128)
        def _(t):
            rows = rows_of(t, 128)
            wide = x_ref[rows, :].astype(F32)
            factor = lax.rsqrt(jnp.mean(wide * wide, axis=-1, keepdims=True) + NORM_EPS)
            fac[rows, :] = factor
            normed = (wide * factor * gain_ref[...]).astype(BF16)
            nrm[rows, :] = normed
            nrm_t[:, rows] = normed.astype(F32).T.astype(BF16)

    def turn(first, second, sign):
        cosine, sine = cos_ref[...], sin_ref[...] * sign
        return first * cosine - second * sine, first * sine + second * cosine

    def project(c):
        mixed = jnp.dot(nrm[...], wq[:, c * COLS : (c + 1) * COLS], preferred_element_type=F32)
        if c == VCHUNK:
            mixed = mixed.astype(BF16).astype(F32)
        mixed_t = mixed.T
        for n in range(COLS // HEAD_DIM):
            at = n * HEAD_DIM
            head = mixed_t[at : at + HEAD_DIM, :]
            if c != VCHUNK:
                first, second = turn(head[: HEAD_DIM // 2], head[HEAD_DIM // 2 :], 1.0)
                head = jnp.concatenate([first, second], axis=0)
            held = head.astype(BF16)
            if c < KCHUNK:
                held = (held.astype(F32) * HEAD_DIM ** (-0.5)).astype(BF16)
            qkv_t[c * COLS + at : c * COLS + at + HEAD_DIM, :] = held
            if c == KCHUNK:
                k_tok[n] = held.astype(F32).T.astype(BF16)
            if c == VCHUNK:
                v_tok[n] = held.astype(F32).T.astype(BF16)

    def project_back():
        @pl.loop(0, 8)
        def _(j):
            rows = rows_of(j, OROWS)
            datt_t[rows, :] = lax.dot_general(
                wo[rows, :], cot_ref[...], NT, preferred_element_type=F32
            ).astype(BF16)

    def attend(g):
        krows = slice(QW + g * HEAD_DIM, QW + (g + 1) * HEAD_DIM)
        vrows = slice(QW + (KV_HEADS + g) * HEAD_DIM, QW + (KV_HEADS + g + 1) * HEAD_DIM)
        dk_acc[...] = jnp.zeros_like(dk_acc)
        dv_acc[...] = jnp.zeros_like(dv_acc)

        @pl.loop(0, GROUP, unroll=2)
        def _(n):
            rows = rows_of(g * GROUP + n, HEAD_DIM)
            for q_at in range(0, TOK, QB):
                keys = q_at + QB
                queries = qkv_t[rows, q_at : q_at + QB]
                scores = jnp.dot(k_tok[g, :keys, :], queries, preferred_element_type=F32)
                key_at = lax.broadcasted_iota(jnp.int32, (QB, QB), 0)
                query_at = lax.broadcasted_iota(jnp.int32, (QB, QB), 1)
                masked = jnp.where(query_at >= key_at, scores[q_at:], -1e30)
                scores = jnp.concatenate([scores[:q_at], masked], axis=0) if q_at else masked
                top = jnp.max(scores, axis=0, keepdims=True)
                raised = jnp.exp(scores - top)
                soft = raised * (1.0 / jnp.sum(raised, axis=0, keepdims=True))
                weights = soft.astype(BF16)
                out = jnp.dot(qkv_t[vrows, :keys], weights, preferred_element_type=F32)
                att_t[rows, q_at : q_at + QB] = out.astype(BF16)
                dout = datt_t[rows, q_at : q_at + QB]
                dweights = jnp.dot(v_tok[g, :keys, :], dout, preferred_element_type=F32)
                dot_out = jnp.sum(out * dout.astype(F32), axis=0, keepdims=True)
                dscores = (soft * (dweights - dot_out)).astype(BF16)
                dqueries = jnp.dot(qkv_t[krows, :keys], dscores, preferred_element_type=F32)
                dqueries = (dqueries * HEAD_DIM ** (-0.5)).astype(BF16).astype(F32)
                half = HEAD_DIM // 2
                cosine, sine = cos_ref[:, q_at : q_at + QB], sin_ref[:, q_at : q_at + QB]
                first, second = dqueries[:half], dqueries[half:]
                dm_t[rows, q_at : q_at + QB] = jnp.concatenate(
                    [first * cosine + second * sine, second * cosine - first * sine], axis=0
                ).astype(BF16)
                dk_acc[:, :keys] += lax.dot_general(queries, dscores, NT, preferred_element_type=F32)
                dv_acc[:, :keys] += lax.dot_general(dout, weights, NT, preferred_element_type=F32)

        dkeys = dk_acc[...].astype(BF16).astype(F32)
        first, second = turn(dkeys[: HEAD_DIM // 2], dkeys[HEAD_DIM // 2 :], -1.0)
        dm_t[krows, :] = jnp.concatenate([first, second], axis=0).astype(BF16)
        dm_t[vrows, :] = dv_acc[...].astype(BF16)

    def gq_block(x_at, z_at, c):
        return gq.at[rows_of(x_at * 2 + z_at, QROWS), pl.ds(c * COLS, COLS)]

    def rq_at(n, c):
        return rq.at[n, :, pl.ds(c * COLS, COLS)]

    def grad_chunk(c):
        cols = slice(c * COLS, (c + 1) * COLS)

        @pl.loop(0, 8)
        def _(j):
            rows = rows_of(j, QROWS)
            gq[rows, cols] = lax.dot_general(
                nrm_t[rows, :], dm_t[cols, :], NT, preferred_element_type=F32
            ).astype(BF16)

        for n, (block, to) in enumerate((
            (gq_block(at_x(2), 0, c), left),
            (gq_block(at_x(2), 1, c), right),
            (gq_block(at_x(3), 1, c), left),
            (gq_block(at_x(1), 0, c), right),
        )):
            send(block, rq_at(n, c), rsq_s.at[c, n], rsq_r.at[c, n], to)
        dm[:, cols] = dm_t[cols, :].astype(F32).T.astype(BF16)

    def add_chunk(c):
        for n, (block, to) in enumerate(((gq_block(at_x(3), 0, c), left), (gq_block(at_x(1), 1, c), right))):
            got(rq_at(n, c), rsq_r.at[c, n])
            block[...] = (block[...].astype(F32) + rq_at(n, c)[...].astype(F32)).astype(BF16)
            send(block, rq_at(4 + n, c), rsq_s.at[c, 4 + n], rsq_r.at[c, 4 + n], to)

    def fold_chunk(c):
        for n in range(2, 6):
            got(rq_at(n, c), rsq_r.at[c, n])

        def whole(z_at, first, second):
            return (
                gq_block(a, z_at, c)[...].astype(F32)
                + rq.at[first, :, pl.ds(c * COLS, COLS)][...].astype(F32)
                + rq.at[second, :, pl.ds(c * COLS, COLS)][...].astype(F32)
            )

        block = gq_block(a, 1 - b, c)
        block[...] = whole(1 - b, 2 + b, 5 - b).astype(BF16)
        send(block, rq_at(6, c), rsq_s.at[c, 6], rsq_r.at[c, 6], across)
        block = gq_block(a, b, c)
        block[...] = whole(b, 3 - b, 4 + b).astype(BF16)

    def end_chunk(c):
        got(rq_at(6, c), rsq_r.at[c, 6])
        cols = pl.ds(c * COLS, COLS)
        sumq_ref[:, cols] = (gq_block(a, b, c)[...].astype(F32) + rq_at(6, c)[...].astype(F32)).astype(BF16)
        store(sumq_ref.at[:, cols], sumq_out.at[:, cols])

    def go_rows(x_at, z_at, half=None):
        start = (x_at * 2 + z_at) * OROWS
        if half is None:
            return go.at[pl.ds(pl.multiple_of(start, OROWS), OROWS)]
        return go.at[pl.ds(pl.multiple_of(start + half * HALF, HALF), HALF)]

    def grad_out(g):
        @pl.loop(0, 2)
        def _(z_at):
            rows = rows_of(2 * g + z_at, OROWS)
            go[rows, :] = jnp.dot(att_t[rows, :], cot_ref[...], preferred_element_type=F32).astype(BF16)

        send(go_rows(g, 1 - b), ro_z.at[g], rso_s.at[6 + g], rso_r.at[6 + g], across)

    def pair_out(step):
        x_at = at_x(step)
        got(ro_z.at[x_at], rso_r.at[6 + x_at])
        block = go_rows(x_at, b)
        block[...] = (block[...].astype(F32) + ro_z[x_at].astype(F32)).astype(BF16)

    def ring_out():
        pair_out(2)
        send(go_rows(at_x(2), b, 0), ro.at[0], rso_s.at[0], rso_r.at[0], left)
        send(go_rows(at_x(2), b, 1), ro.at[1], rso_s.at[1], rso_r.at[1], right)
        pair_out(3)
        send(go_rows(at_x(3), b, 1), ro.at[2], rso_s.at[2], rso_r.at[2], left)
        pair_out(1)
        send(go_rows(at_x(1), b, 0), ro.at[3], rso_s.at[3], rso_r.at[3], right)
        pair_out(0)

    def add_out():
        for n, (block, to) in enumerate(((go_rows(at_x(3), b, 0), left), (go_rows(at_x(1), b, 1), right))):
            got(ro.at[n], rso_r.at[n])
            block[...] = (block[...].astype(F32) + ro[n].astype(F32)).astype(BF16)
            send(block, ro.at[4 + n], rso_s.at[4 + n], rso_r.at[4 + n], to)

    def end_out():
        for n in range(2, 6):
            got(ro.at[n], rso_r.at[n])
        for half, (first, second) in enumerate(((3, 4), (2, 5))):
            sumo_ref[half * HALF : (half + 1) * HALF, :] = (
                go_rows(a, b, half)[...].astype(F32) + ro[first].astype(F32) + ro[second].astype(F32)
            ).astype(BF16)
        store(sumo_ref, sumo_out)

    def gain_grad():
        @pl.loop(0, 8)
        def _(j):
            dnormed = lax.dot_general(
                dm[...], wq[rows_of(j, QROWS), :], NT, preferred_element_type=F32
            ).astype(BF16).astype(F32)
            wide = x_ref[:, rows_of(j, QROWS)].astype(F32) * fac[...]
            g_rows[pl.ds(j, 1), :] = jnp.sum(dnormed * wide, axis=0, keepdims=True)

        @pl.loop(1, 8)
        def _(step):
            pltpu.make_async_remote_copy(
                src_ref=g_rows, dst_ref=g_recv.at[f], send_sem=gg_s.at[step], recv_sem=gg_r.at[step],
                device_id={"fsdp": lax.rem(f + step, 8)}, device_id_type=MESH,
            ).start()
        g_recv[f] = g_rows[...]

    def gain_sum():
        @pl.loop(1, 8)
        def _(step):
            got(g_recv.at[lax.rem(f - step + 8, 8)], gg_r.at[step])
        total = g_recv[0]
        for i in range(1, 8):
            total = total + g_recv[i]
        for i in range(8):
            sumg_ref[:, i * 256 : (i + 1) * 256] = total[i : i + 1, :]
        store(sumg_ref, sumg_out)

        @pl.loop(1, 8)
        def _(step):
            left_here(g_rows, gg_s.at[step])

    chunks[KCHUNK].own()
    out_paired.own()
    out_ringed.own()
    chunks[VCHUNK].own()
    chunks[0].own()
    chunks[KCHUNK].pair()
    for copy in loads[:6]:
        copy.wait()
    out_paired.pair()
    island_start()
    chunks[VCHUNK].pair()
    normalise()
    for copy in loads[6:]:
        copy.wait()
    out_ringed.onward()
    chunks[0].pair()
    island_ring()
    chunks[KCHUNK].onward()
    chunks[1].own()
    chunks[2].own()
    chunks[3].own()
    out_paired.onward()
    out_ringed.far()
    chunks[VCHUNK].onward()
    island_far()
    chunks[0].onward()
    chunks[KCHUNK].have()
    project(KCHUNK)
    chunks[1].pair()
    chunks[2].pair()
    island_sum()
    chunks[VCHUNK].have()
    project(VCHUNK)
    chunks[3].onward()
    back_ring()
    out_paired.have()
    out_ringed.have()
    project_back()
    chunks[0].have()
    project(0)
    back_core()
    attend(0)
    grad_chunk(0)
    chunks[1].onward()
    chunks[2].onward()
    chunks[3].far()
    grad_out(0)
    chunks[1].have()
    project(1)
    attend(1)
    grad_chunk(1)
    add_chunk(0)
    grad_out(1)
    chunks[2].have()
    project(2)
    attend(2)
    grad_chunk(2)
    add_chunk(1)
    grad_out(2)
    fold_chunk(0)
    chunks[3].have()
    project(3)
    attend(3)
    grad_chunk(3)
    grad_chunk(KCHUNK)
    grad_chunk(VCHUNK)
    add_chunk(2)
    grad_out(3)
    fold_chunk(1)
    add_chunk(3)
    fold_chunk(2)
    ring_out()
    add_chunk(KCHUNK)
    fold_chunk(3)
    add_chunk(VCHUNK)
    add_out()
    gain_grad()
    end_chunk(0)
    end_chunk(1)
    fold_chunk(KCHUNK)
    island_whole()
    fold_chunk(VCHUNK)
    end_chunk(2)
    end_chunk(3)
    end_out()
    end_chunk(KCHUNK)
    gain_sum()
    end_chunk(VCHUNK)
    for copy in stores:
        copy.wait()
    for src, s_sem in sent:
        left_here(src, s_sem)


def grads(islands, x, cot, gain, wq, wo, qglob, qmom, oglob, omom):
    qshare, oshare = QKV // islands, D // islands
    cosine, sine = rope_tables()
    hbm = pl.BlockSpec(memory_space=pl.ANY)
    dma = pltpu.SemaphoreType.DMA
    operands = (x, cot, gain, wq, wo, jnp.asarray(cosine), jnp.asarray(sine), qglob, qmom, oglob, omom)
    results = [
        jax.ShapeDtypeStruct((QROWS, QKV), BF16),
        jax.ShapeDtypeStruct((OROWS, D), BF16),
        jax.ShapeDtypeStruct((1, D), F32),
        jax.ShapeDtypeStruct((qshare, QROWS), F32),
        jax.ShapeDtypeStruct((OROWS, oshare), F32),
        jax.ShapeDtypeStruct((1, D), F32),
        jax.ShapeDtypeStruct((QROWS, QKV), BF16),
        jax.ShapeDtypeStruct((OROWS, D), BF16),
    ]
    return pl.pallas_call(
        functools.partial(grads_kernel, islands),
        out_shape=results,
        in_specs=[hbm] * 11,
        out_specs=[hbm] * 8,
        scratch_shapes=[
            *(pltpu.VMEM(operands[n].shape, operands[n].dtype) for n in (0, 1, 2, 5, 6, 7, 8, 9, 10)),
            *(pltpu.VMEM(r.shape, r.dtype) for r in results),
            pltpu.VMEM((D, QKV), BF16),
            pltpu.VMEM((QW, D), BF16),
            pltpu.VMEM((TOK, D), BF16),
            pltpu.VMEM((D, TOK), BF16),
            pltpu.VMEM((TOK, 1), F32),
            pltpu.VMEM((QKV, TOK), BF16),
            pltpu.VMEM((KV_HEADS, TOK, HEAD_DIM), BF16),
            pltpu.VMEM((KV_HEADS, TOK, HEAD_DIM), BF16),
            pltpu.VMEM((QW, TOK), BF16),
            pltpu.VMEM((QW, TOK), BF16),
            pltpu.VMEM((QKV, TOK), BF16),
            pltpu.VMEM((TOK, QKV), BF16),
            pltpu.VMEM((HEAD_DIM, TOK), F32),
            pltpu.VMEM((HEAD_DIM, TOK), F32),
            pltpu.VMEM((D, QKV), BF16),
            pltpu.VMEM((QW, D), BF16),
            pltpu.VMEM((7, QROWS, QKV), BF16),
            pltpu.VMEM((6, HALF, D), BF16),
            pltpu.VMEM((4, OROWS, D), BF16),
            pltpu.VMEM((8, 256), F32),
            pltpu.VMEM((8, 8, 256), F32),
            pltpu.VMEM((8, 2, qshare, QROWS), BF16),
            pltpu.VMEM((8, 2, OROWS, oshare), BF16),
            pltpu.VMEM((8, qshare, QROWS), BF16),
            pltpu.VMEM((8, OROWS, oshare), BF16),
            pltpu.VMEM((8, 256), F32),
            pltpu.VMEM((4, 2, qshare, QROWS), BF16),
            pltpu.VMEM((4, 2, OROWS, oshare), BF16),
            pltpu.VMEM((4, 8, 256), F32),
            pltpu.VMEM((qshare, QROWS), BF16),
            pltpu.VMEM((OROWS, oshare), BF16),
            pltpu.VMEM((8, 256), F32),
            pltpu.VMEM((8, 256), F32),
            pltpu.VMEM((8, 2, qshare, QROWS), BF16),
            pltpu.VMEM((8, 2, OROWS, oshare), BF16),
            dma((11,)),
            dma((13,)),
            dma((CHUNKS, 7)), dma((CHUNKS, 7)),
            dma((2, 9)), dma((2, 9)),
            dma((CHUNKS, 7)), dma((CHUNKS, 7)),
            dma((10,)), dma((10,)),
            dma((8,)), dma((8,)),
            dma((25,)), dma((25,)),
        ],
        compiler_params=pltpu.CompilerParams(
            collective_id=0, has_side_effects=True, vmem_limit_bytes=63 * 2**20
        ),
        name="grads",
    )(*operands)


PARTS = 4


def update_kernel(islands, *refs):
    (
        gain_ref, wq_in, wo_in, gf_ref, gs_ref, qf_in, qs_in, of_in, os_in,
        gg_ref, gm_ref, qg_ref, qm_ref, og_ref, om_ref,
        sumq_in, sumo_in, sumg_ref, totq_ref, toto_ref, totg_ref, wholeq_in, wholeo_in,
        gain_o, wq_out, wo_out, gf_o, gs_o, qf_out, qs_out, of_out, os_out,
        gg_o, gm_o, qg_o, qm_o, og_o, om_o,
        *scratch, in_sem, out_sem,
    ) = refs
    sources = (wq_in, sumq_in, qf_in, qs_in, wholeq_in, wo_in, sumo_in, of_in, os_in, wholeo_in)
    targets = (wq_out, qf_out, qs_out, wo_out, of_out, os_out)
    held, made = scratch[: len(sources)], scratch[len(sources) :]

    def part(ref, i):
        size = ref.shape[0] // PARTS
        return ref.at[pl.ds(i * size, size)]

    loads = [
        [pltpu.make_async_copy(part(src, i), part(dst, i), in_sem.at[i, n]) for n, (src, dst) in enumerate(zip(sources, held))]
        for i in range(PARTS)
    ]
    for row in loads:
        for copy in row:
            copy.start()
    scale = 1.0 / islands
    stepped, first, second = adamw(gain_ref[...], sumg_ref[...], gf_ref[...], gs_ref[...], 0.0)
    outer, momentum = nesterov(gg_ref[...], gm_ref[...], totg_ref[...] * scale)
    gain_o[...] = MIXING * stepped + (1.0 - MIXING) * outer
    gf_o[...] = first
    gs_o[...] = second
    gg_o[...] = outer
    gm_o[...] = momentum
    qg_o[...], qm_o[...] = nesterov(qg_ref[...], qm_ref[...], totq_ref[...] * scale)
    og_o[...], om_o[...] = nesterov(og_ref[...], om_ref[...], toto_ref[...] * scale)
    stores = []
    for i in range(PARTS):
        for copy in loads[i]:
            copy.wait()
        for which in range(2):
            w, s, m1, m2, whole = (part(ref, i) for ref in held[5 * which : 5 * which + 5])
            outs = [part(ref, i) for ref in made[3 * which : 3 * which + 3]]
            stepped, first, second = adamw(w[...], s[...].astype(F32), m1[...], m2[...], WEIGHT_DECAY)
            outs[0][...] = (MIXING * stepped + (1.0 - MIXING) * whole[...].astype(F32)).astype(BF16)
            outs[1][...] = first
            outs[2][...] = second
            for n in range(3):
                copy = pltpu.make_async_copy(
                    outs[n], part(targets[3 * which + n], i), out_sem.at[i, 3 * which + n]
                )
                copy.start()
                stores.append(copy)
    for copy in stores:
        copy.wait()


def update(islands, state, sums):
    def spec(array):
        big = array.shape in ((QROWS, QKV), (OROWS, D))
        return pl.BlockSpec(memory_space=pl.ANY if big else pltpu.VMEM)

    def room(*arrays):
        return [pltpu.VMEM(v.shape, v.dtype) for v in arrays]

    return pl.pallas_call(
        functools.partial(update_kernel, islands),
        out_shape=[jax.ShapeDtypeStruct(o.shape, o.dtype) for o in state],
        in_specs=[spec(v) for v in (*state, *sums)],
        out_specs=[spec(o) for o in state],
        scratch_shapes=[
            *room(state[1], sums[0], state[5], state[6], sums[6], state[2], sums[1], state[7], state[8], sums[7]),
            *room(state[1], state[5], state[6], state[2], state[7], state[8]),
            pltpu.SemaphoreType.DMA((PARTS, 10)),
            pltpu.SemaphoreType.DMA((PARTS, 6)),
        ],
        compiler_params=pltpu.CompilerParams(vmem_limit_bytes=60 * 2**20),
        name="update",
    )(*state, *sums)


def shards(
    tokens, cotangent, norm_gain, qkv_weight, out_weight, gain_first, gain_second,
    qkv_first, qkv_second, out_first, out_second,
    gain_global, gain_momentum, qkv_global, qkv_momentum, out_global, out_momentum,
):
    islands = lax.axis_size("island")
    wq, wo = qkv_weight[0], out_weight[0]
    qkv_global, qkv_momentum = qkv_global.T, qkv_momentum.T
    sums = grads(
        islands, tokens, cotangent, norm_gain, wq, wo, qkv_global, qkv_momentum, out_global, out_momentum
    )
    state = (
        norm_gain, wq, wo, gain_first, gain_second, qkv_first[0], qkv_second[0], out_first[0], out_second[0],
        gain_global[None], gain_momentum[None], qkv_global, qkv_momentum, out_global, out_momentum,
    )
    (
        gain_next, wq_next, wo_next, gf, gs, qf, qs, of, os_, gg, gm, qg, qm, og, om
    ) = update(islands, state, sums)
    return (
        gain_next, wq_next[None], wo_next[None], gf, gs, qf[None], qs[None], of[None], os_[None],
        gg[0], gm[0], qg.T, qm.T, og, om,
    )


def solution(mesh):
    placed = (
        P(("island", "fsdp"), None),
        P(("island", "fsdp"), None),
        P("island", None),
        P("island", "fsdp", None),
        P("island", "fsdp", None),
        P("island", None),
        P("island", None),
        P("island", "fsdp", None),
        P("island", "fsdp", None),
        P("island", "fsdp", None),
        P("island", "fsdp", None),
        P(),
        P(),
        P("fsdp", "island"),
        P("fsdp", "island"),
        P("fsdp", "island"),
        P("fsdp", "island"),
    )
    return jax.shard_map(
        shards,
        mesh=mesh,
        in_specs=placed,
        out_specs=(
            P("island", None),
            P("island", "fsdp", None),
            P("island", "fsdp", None),
            P("island", None),
            P("island", None),
            P("island", "fsdp", None),
            P("island", "fsdp", None),
            P("island", "fsdp", None),
            P("island", "fsdp", None),
            P(),
            P(),
            P("fsdp", "island"),
            P("fsdp", "island"),
            P("fsdp", "island"),
            P("fsdp", "island"),
        ),
        check_vma=False,
    )
```

```python
import functools

import jax
import jax.numpy as jnp
import numpy as np
from jax import lax
from jax.experimental import pallas as pl
from jax.experimental.pallas import tpu as pltpu
from jax.sharding import PartitionSpec as P

HEADS = 16
KV_HEADS = 4
HEAD_DIM = 64
GROUP = HEADS // KV_HEADS

BETA_ONE = 0.9
BETA_TWO = 0.95
ADAM_EPS = 1e-08
INNER_RATE = 0.001
WEIGHT_DECAY = 0.1
STEP_COUNT = 100.0
OUTER_RATE = 0.7
OUTER_MOMENTUM = 0.9
MIXING = 0.5
NORM_EPS = 1e-05
ROPE_BASE = 500000.0

MESH = pl.DeviceIdType.MESH
F32 = jnp.float32
BF16 = jnp.bfloat16

TOK = 512
D = 2048
QW = HEADS * HEAD_DIM
QKV = QW + 2 * KV_HEADS * HEAD_DIM
QROWS = 256
OROWS = 128
HALF = OROWS // 2
OPAIRED = 896
COLS = 256
CHUNKS = QKV // COLS
KCHUNK, VCHUNK = QW // COLS, QW // COLS + 1
QB = 512
NT = (((1,), (1,)), ((), ()))


def rope_tables():
    half = HEAD_DIM // 2
    freqs = ROPE_BASE ** (-np.arange(half, dtype=np.float64) / half)
    angles = freqs[:, None] * np.arange(TOK, dtype=np.float64)[None, :]
    return np.cos(angles).astype(np.float32), np.sin(angles).astype(np.float32)


def adamw(param, grad, first, second, decay):
    wide = param.astype(F32)
    first_next = BETA_ONE * first + (1.0 - BETA_ONE) * grad
    second_next = BETA_TWO * second + (1.0 - BETA_TWO) * grad * grad
    update = (
        first_next
        * (1.0 / (1.0 - BETA_ONE**STEP_COUNT))
        / (jnp.sqrt(second_next * (1.0 / (1.0 - BETA_TWO**STEP_COUNT))) + ADAM_EPS)
    )
    return (wide - INNER_RATE * (update + decay * wide), first_next, second_next)


def nesterov(global_value, momentum, average):
    delta = global_value - average
    momentum_next = OUTER_MOMENTUM * momentum + delta
    return (global_value - OUTER_RATE * (delta + OUTER_MOMENTUM * momentum_next), momentum_next)


def rows_of(index, size):
    return pl.ds(pl.multiple_of(index * size, size), size)


def grads_kernel(
    islands,
    x_in, cot_in, gain_in, wq_in, wo_in, cos_in, sin_in, qglob_in, qmom_in, oglob_in, omom_in,
    sumq_out, sumo_out, sumg_out, totq_out, toto_out, totg_out, wholeq_out, wholeo_out,
    x_ref, cot_ref, gain_ref, cos_ref, sin_ref, qglob_ref, qmom_ref, oglob_ref, omom_ref,
    sumq_ref, sumo_ref, sumg_ref, totq_ref, toto_ref, totg_ref, wholeq_ref, wholeo_ref,
    wq, wo, nrm, nrm_t, fac, qkv_t, k_tok, v_tok, datt_t, att_t, dm_t, dm, dk_acc, dv_acc,
    gq, go, rq, ro, ro_z, g_rows, g_recv,
    i_own, io_own, i_core, io_core, ig_core, i_ring, io_ring, ig_ring, i_far, io_far, ig_far, ig_own, i_back, io_back,
    own_sem, out_sem, agq_s, agq_r, ago_s, ago_r, rsq_s, rsq_r, rso_s, rso_r, gg_s, gg_r, is_s, is_r,
):
    f = lax.axis_index("fsdp")
    me = lax.axis_index("island")
    a, b = f // 2, f % 2
    y, zh, core = me // 4, (me // 2) % 2, me % 2
    qshare = QKV // islands
    oshare = D // islands

    def at_x(step):
        return lax.rem(a + step, 4)

    right = {"fsdp": at_x(1) * 2 + b}
    left = {"fsdp": at_x(3) * 2 + b}
    across = {"fsdp": a * 2 + 1 - b}
    sent = []

    def send(src, dst, s_sem, r_sem, to):
        copy = pltpu.make_async_remote_copy(
            src_ref=src, dst_ref=dst, send_sem=s_sem, recv_sem=r_sem, device_id=to, device_id_type=MESH
        )
        copy.start()
        sent.append((src, s_sem))

    def got(dst, r_sem):
        pltpu.make_async_remote_copy(
            src_ref=dst, dst_ref=dst, send_sem=r_sem, recv_sem=r_sem, device_id=across, device_id_type=MESH
        ).wait_recv()

    def left_here(src, s_sem):
        pltpu.make_async_remote_copy(
            src_ref=src, dst_ref=src, send_sem=s_sem, recv_sem=s_sem, device_id=across, device_id_type=MESH
        ).wait_send()

    barrier = pltpu.get_barrier_semaphore()

    @pl.loop(1, 8)
    def _(step):
        pl.semaphore_signal(barrier, inc=1, device_id={"fsdp": lax.rem(f + step, 8)}, device_id_type=MESH)

    other_core = {"island": me + 1 - 2 * core}
    other_far = {"island": me + 2 - 4 * zh}

    def other_y(step):
        return lax.rem(y + step, 4)

    def on_y(step):
        return {"island": other_y(step) * 4 + zh * 2 + core}

    pl.semaphore_signal(barrier, inc=1, device_id=other_core, device_id_type=MESH)
    pl.semaphore_signal(barrier, inc=1, device_id=other_far, device_id_type=MESH)
    for step in range(1, 4):
        pl.semaphore_signal(barrier, inc=1, device_id=on_y(step), device_id_type=MESH)
    loads = [
        pltpu.make_async_copy(src, dst, own_sem.at[n])
        for n, (src, dst) in enumerate((
            (x_in, x_ref), (gain_in, gain_ref), (wq_in, wq.at[rows_of(f, QROWS)]), (wo_in, wo.at[rows_of(f, OROWS)]),
            (cos_in, cos_ref), (sin_in, sin_ref), (cot_in, cot_ref), (qglob_in, qglob_ref), (qmom_in, qmom_ref),
            (oglob_in, oglob_ref), (omom_in, omom_ref),
        ))
    ]
    for copy in loads:
        copy.start()
    stores = []

    def store(src, dst):
        copy = pltpu.make_async_copy(src, dst, out_sem.at[len(stores)])
        copy.start()
        stores.append(copy)

    pl.semaphore_wait(barrier, 7 + 5)

    def wq_block(c):
        def block(x_at, z_at, half=None):
            start, size = (x_at * 2 + z_at) * QROWS, QROWS
            if half is not None:
                start, size = start + half * (QROWS // 2), QROWS // 2
            return wq.at[pl.ds(pl.multiple_of(start, size), size), pl.ds(c * COLS, COLS)]

        return block

    def wo_block(col, cols):
        def block(x_at, z_at, half=None):
            start, size = (x_at * 2 + z_at) * OROWS, OROWS
            if half is not None:
                start, size = start + half * HALF, HALF
            return wo.at[pl.ds(pl.multiple_of(start, size), size), pl.ds(col, cols)]

        return block

    class Paired:
        def __init__(self, src, block, n):
            self.src, self.block, self.s, self.r = src, block, agq_s.at[n], agq_r.at[n]

        def own(self):
            dst = self.block(a, b)
            send(self.src, dst, self.s.at[0], self.r.at[0], across)
            send(self.src, dst, self.s.at[1], self.r.at[1 + b], right)
            send(self.src, dst, self.s.at[2], self.r.at[3 + b], left)

        def pair(self):
            block = self.block(a, 1 - b)
            got(block, self.r.at[0])
            send(block, block, self.s.at[3], self.r.at[1 + 1 - b], right)
            send(block, block, self.s.at[4], self.r.at[3 + 1 - b], left)

        def onward(self):
            block = self.block(at_x(3), 1)
            got(block, self.r.at[2])
            send(block, block, self.s.at[5], self.r.at[5], right)
            block = self.block(at_x(1), 0)
            got(block, self.r.at[3])
            send(block, block, self.s.at[6], self.r.at[6], left)

        def have(self):
            got(self.block(at_x(3), 0), self.r.at[1])
            got(self.block(at_x(1), 1), self.r.at[4])
            got(self.block(at_x(2), 1), self.r.at[5])
            got(self.block(at_x(2), 0), self.r.at[6])

    class Ringed:
        def __init__(self, src, block, n):
            self.src, self.block, self.s, self.r = src, block, ago_s.at[n], ago_r.at[n]

        def own(self):
            dst = self.block(a, b)
            send(self.src, dst, self.s.at[0], self.r.at[0], right)
            send(self.src, dst, self.s.at[1], self.r.at[1], left)
            send(self.src, dst, self.s.at[2], self.r.at[2], across)

        def onward(self):
            for n, (x_at, to) in enumerate(((at_x(3), right), (at_x(1), left))):
                block, part = self.block(x_at, b), self.block(x_at, b, n)
                got(block, self.r.at[n])
                send(part, part, self.s.at[3 + n], self.r.at[3 + n], to)
                send(block, block, self.s.at[5 + n], self.r.at[5 + n], across)

        def far(self):
            for n in range(2):
                part = self.block(at_x(2), b, n)
                got(part, self.r.at[3 + n])
                send(part, part, self.s.at[7 + n], self.r.at[7 + n], across)

        def have(self):
            got(self.block(a, 1 - b), self.r.at[2])
            got(self.block(at_x(3), 1 - b), self.r.at[5])
            got(self.block(at_x(1), 1 - b), self.r.at[6])
            for n in range(2):
                got(self.block(at_x(2), 1 - b, n), self.r.at[7 + n])

    chunks = [
        (Paired if c != 3 else Ringed)(wq_in.at[:, pl.ds(c * COLS, COLS)], wq_block(c), c if c != 3 else 1)
        for c in range(CHUNKS)
    ]
    out_paired = Paired(wo_in.at[:, pl.ds(0, OPAIRED)], wo_block(0, OPAIRED), 3)
    out_ringed = Ringed(wo_in.at[:, pl.ds(OPAIRED, D - OPAIRED)], wo_block(OPAIRED, D - OPAIRED), 0)

    def island_start():
        own = wq.at[rows_of(f, QROWS)]
        for i in range(islands):
            if i % 4 == 0:
                turned = own[:, i * qshare : (i + 4) * qshare].astype(F32).T.astype(BF16)
            i_own[i // 2, i % 2] = turned[i % 4 * qshare : (i % 4 + 1) * qshare]
            io_own[i // 2, i % 2] = wo[rows_of(f, OROWS), i * oshare : (i + 1) * oshare]
        for i in range(8):
            ig_own[i : i + 1, :] = gain_ref[:, i * 256 : (i + 1) * 256]
        send(i_own.at[:, 1 - core], i_core, is_s.at[0], is_r.at[0], other_core)
        send(io_own.at[:, 1 - core], io_core, is_s.at[1], is_r.at[1], other_core)
        send(ig_own, ig_core, is_s.at[2], is_r.at[2], other_core)

    def island_ring():
        got(i_core, is_r.at[0])
        got(io_core, is_r.at[1])
        got(ig_core, is_r.at[2])

        @pl.loop(0, 8)
        def _(n):
            i_core[n] = (i_core[n].astype(F32) + i_own[n, core].astype(F32)).astype(BF16)
            io_core[n] = (io_core[n].astype(F32) + io_own[n, core].astype(F32)).astype(BF16)

        ig_core[...] += ig_own[...]
        for step in range(1, 4):
            two = pl.ds(other_y(step) * 2, 2)
            send(i_core.at[two], i_ring.at[y], is_s.at[3 * step], is_r.at[3 * step], on_y(step))
            send(io_core.at[two], io_ring.at[y], is_s.at[3 * step + 1], is_r.at[3 * step + 1], on_y(step))
            send(ig_core, ig_ring.at[y], is_s.at[3 * step + 2], is_r.at[3 * step + 2], on_y(step))
        two = pl.ds(y * 2, 2)
        i_ring[y] = i_core[two]
        io_ring[y] = io_core[two]
        ig_ring[y] = ig_core[...]

    def island_far():
        for step in range(1, 4):
            source = other_y(4 - step)
            got(i_ring.at[source], is_r.at[3 * step])
            got(io_ring.at[source], is_r.at[3 * step + 1])
            got(ig_ring.at[source], is_r.at[3 * step + 2])
        i_ring[0] = (
            i_ring[0].astype(F32) + i_ring[1].astype(F32) + i_ring[2].astype(F32) + i_ring[3].astype(F32)
        ).astype(BF16)
        io_ring[0] = (
            io_ring[0].astype(F32) + io_ring[1].astype(F32) + io_ring[2].astype(F32) + io_ring[3].astype(F32)
        ).astype(BF16)
        ig_ring[0] = ig_ring[0] + ig_ring[1] + ig_ring[2] + ig_ring[3]
        send(i_ring.at[0, 1 - zh], i_far, is_s.at[12], is_r.at[12], other_far)
        send(io_ring.at[0, 1 - zh], io_far, is_s.at[13], is_r.at[13], other_far)
        send(ig_ring.at[0], ig_far, is_s.at[14], is_r.at[14], other_far)

    def island_sum():
        got(i_far, is_r.at[12])
        got(io_far, is_r.at[13])
        got(ig_far, is_r.at[14])
        totq_ref[...] = i_ring[0, zh].astype(F32) + i_far[...].astype(F32)
        toto_ref[...] = io_ring[0, zh].astype(F32) + io_far[...].astype(F32)
        total = ig_ring[0] + ig_far[...]
        for i in range(8):
            totg_ref[:, i * 256 : (i + 1) * 256] = total[i : i + 1, :]
        here = me // 2
        i_back[here, core] = nesterov(
            qglob_ref[...], qmom_ref[...], totq_ref[...] * (1.0 / islands)
        )[0].astype(BF16)
        io_back[here, core] = nesterov(
            oglob_ref[...], omom_ref[...], toto_ref[...] * (1.0 / islands)
        )[0].astype(BF16)
        send(i_back.at[here, core], i_back.at[here, core], is_s.at[15], is_r.at[15], other_far)
        send(io_back.at[here, core], io_back.at[here, core], is_s.at[16], is_r.at[16], other_far)
        store(totq_ref, totq_out)
        store(toto_ref, toto_out)
        store(totg_ref, totg_out)

    def back_ring():
        there = y * 2 + 1 - zh
        got(i_back.at[there, core], is_r.at[15])
        got(io_back.at[there, core], is_r.at[16])
        mine = i_back.at[pl.ds(y * 2, 2), core], io_back.at[pl.ds(y * 2, 2), core]
        for step in range(1, 4):
            for n in range(2):
                at = 17 + 2 * (step - 1) + n
                send(mine[n], mine[n], is_s.at[at], is_r.at[at], on_y(step))

    def back_core():
        for step in range(1, 4):
            source = pl.ds(other_y(4 - step) * 2, 2)
            got(i_back.at[source, core], is_r.at[17 + 2 * (step - 1)])
            got(io_back.at[source, core], is_r.at[18 + 2 * (step - 1)])
        send(i_back.at[:, core], i_back.at[:, core], is_s.at[23], is_r.at[23], other_core)
        send(io_back.at[:, core], io_back.at[:, core], is_s.at[24], is_r.at[24], other_core)

    def island_whole():
        got(i_back.at[:, 1 - core], is_r.at[23])
        got(io_back.at[:, 1 - core], is_r.at[24])
        for i in range(islands // 4):
            four = jnp.concatenate([i_back[2 * i + n // 2, n % 2] for n in range(4)], axis=0)
            wholeq_ref[:, i * 4 * qshare : (i + 1) * 4 * qshare] = four.astype(F32).T.astype(BF16)
        for i in range(islands):
            wholeo_ref[:, i * oshare : (i + 1) * oshare] = io_back[i // 2, i % 2]
        store(wholeq_ref, wholeq_out)
        store(wholeo_ref, wholeo_out)

    def normalise():
        @pl.loop(0, TOK // 128)
        def _(t):
            rows = rows_of(t, 128)
            wide = x_ref[rows, :].astype(F32)
            factor = lax.rsqrt(jnp.mean(wide * wide, axis=-1, keepdims=True) + NORM_EPS)
            fac[rows, :] = factor
            normed = (wide * factor * gain_ref[...]).astype(BF16)
            nrm[rows, :] = normed
            nrm_t[:, rows] = normed.astype(F32).T.astype(BF16)

    def turn(first, second, sign):
        cosine, sine = cos_ref[...], sin_ref[...] * sign
        return first * cosine - second * sine, first * sine + second * cosine

    def project(c):
        mixed = jnp.dot(nrm[...], wq[:, c * COLS : (c + 1) * COLS], preferred_element_type=F32)
        if c == VCHUNK:
            mixed = mixed.astype(BF16).astype(F32)
        mixed_t = mixed.T
        for n in range(COLS // HEAD_DIM):
            at = n * HEAD_DIM
            head = mixed_t[at : at + HEAD_DIM, :]
            if c != VCHUNK:
                first, second = turn(head[: HEAD_DIM // 2], head[HEAD_DIM // 2 :], 1.0)
                head = jnp.concatenate([first, second], axis=0)
            held = head.astype(BF16)
            if c < KCHUNK:
                held = (held.astype(F32) * HEAD_DIM ** (-0.5)).astype(BF16)
            qkv_t[c * COLS + at : c * COLS + at + HEAD_DIM, :] = held
            if c == KCHUNK:
                k_tok[n] = held.astype(F32).T.astype(BF16)
            if c == VCHUNK:
                v_tok[n] = held.astype(F32).T.astype(BF16)

    def project_back():
        @pl.loop(0, 2)
        def _(j):
            rows = rows_of(j, QW // 2)
            datt_t[rows, :] = lax.dot_general(
                wo[rows, :], cot_ref[...], NT, preferred_element_type=F32
            ).astype(BF16)

    def attend(g):
        krows = slice(QW + g * HEAD_DIM, QW + (g + 1) * HEAD_DIM)
        vrows = slice(QW + (KV_HEADS + g) * HEAD_DIM, QW + (KV_HEADS + g + 1) * HEAD_DIM)
        dk_acc[...] = jnp.zeros_like(dk_acc)
        dv_acc[...] = jnp.zeros_like(dv_acc)

        @pl.loop(0, GROUP, unroll=2)
        def _(n):
            rows = rows_of(g * GROUP + n, HEAD_DIM)
            for q_at in range(0, TOK, QB):
                keys = q_at + QB
                queries = qkv_t[rows, q_at : q_at + QB]
                scores = jnp.dot(k_tok[g, :keys, :], queries, preferred_element_type=F32)
                key_at = lax.broadcasted_iota(jnp.int32, (QB, QB), 0)
                query_at = lax.broadcasted_iota(jnp.int32, (QB, QB), 1)
                masked = jnp.where(query_at >= key_at, scores[q_at:], -1e30)
                scores = jnp.concatenate([scores[:q_at], masked], axis=0) if q_at else masked
                top = jnp.max(scores, axis=0, keepdims=True)
                raised = jnp.exp(scores - top)
                soft = raised * (1.0 / jnp.sum(raised, axis=0, keepdims=True))
                weights = soft.astype(BF16)
                out = jnp.dot(qkv_t[vrows, :keys], weights, preferred_element_type=F32)
                att_t[rows, q_at : q_at + QB] = out.astype(BF16)
                dout = datt_t[rows, q_at : q_at + QB]
                dweights = jnp.dot(v_tok[g, :keys, :], dout, preferred_element_type=F32)
                dot_out = jnp.sum(out * dout.astype(F32), axis=0, keepdims=True)
                dscores = (soft * (dweights - dot_out)).astype(BF16)
                dqueries = jnp.dot(qkv_t[krows, :keys], dscores, preferred_element_type=F32)
                dqueries = (dqueries * HEAD_DIM ** (-0.5)).astype(BF16).astype(F32)
                half = HEAD_DIM // 2
                cosine, sine = cos_ref[:, q_at : q_at + QB], sin_ref[:, q_at : q_at + QB]
                first, second = dqueries[:half], dqueries[half:]
                dm_t[rows, q_at : q_at + QB] = jnp.concatenate(
                    [first * cosine + second * sine, second * cosine - first * sine], axis=0
                ).astype(BF16)
                dk_acc[:, :keys] += lax.dot_general(queries, dscores, NT, preferred_element_type=F32)
                dv_acc[:, :keys] += lax.dot_general(dout, weights, NT, preferred_element_type=F32)

        dkeys = dk_acc[...].astype(BF16).astype(F32)
        first, second = turn(dkeys[: HEAD_DIM // 2], dkeys[HEAD_DIM // 2 :], -1.0)
        dm_t[krows, :] = jnp.concatenate([first, second], axis=0).astype(BF16)
        dm_t[vrows, :] = dv_acc[...].astype(BF16)

    def gq_block(x_at, z_at, c):
        return gq.at[rows_of(x_at * 2 + z_at, QROWS), pl.ds(c * COLS, COLS)]

    def rq_at(n, c):
        return rq.at[n, :, pl.ds(c * COLS, COLS)]

    def grad_chunk(c):
        cols = slice(c * COLS, (c + 1) * COLS)

        dm[:, cols] = dm_t[cols, :].astype(F32).T.astype(BF16)

        @pl.loop(0, 2)
        def _(j):
            rows = rows_of(j, D // 2)
            gq[rows, cols] = jnp.dot(nrm_t[rows, :], dm[:, cols], preferred_element_type=F32).astype(BF16)

        for n, (block, to) in enumerate((
            (gq_block(at_x(2), 0, c), left),
            (gq_block(at_x(2), 1, c), right),
            (gq_block(at_x(3), 1, c), left),
            (gq_block(at_x(1), 0, c), right),
        )):
            send(block, rq_at(n, c), rsq_s.at[c, n], rsq_r.at[c, n], to)

    def add_chunk(c):
        for n, (block, to) in enumerate(((gq_block(at_x(3), 0, c), left), (gq_block(at_x(1), 1, c), right))):
            got(rq_at(n, c), rsq_r.at[c, n])
            block[...] = (block[...].astype(F32) + rq_at(n, c)[...].astype(F32)).astype(BF16)
            send(block, rq_at(4 + n, c), rsq_s.at[c, 4 + n], rsq_r.at[c, 4 + n], to)

    def fold_chunk(c):
        for n in range(2, 6):
            got(rq_at(n, c), rsq_r.at[c, n])

        def whole(z_at, first, second):
            return (
                gq_block(a, z_at, c)[...].astype(F32)
                + rq.at[first, :, pl.ds(c * COLS, COLS)][...].astype(F32)
                + rq.at[second, :, pl.ds(c * COLS, COLS)][...].astype(F32)
            )

        block = gq_block(a, 1 - b, c)
        block[...] = whole(1 - b, 2 + b, 5 - b).astype(BF16)
        send(block, rq_at(6, c), rsq_s.at[c, 6], rsq_r.at[c, 6], across)
        block = gq_block(a, b, c)
        block[...] = whole(b, 3 - b, 4 + b).astype(BF16)

    def end_chunk(c):
        got(rq_at(6, c), rsq_r.at[c, 6])
        cols = pl.ds(c * COLS, COLS)
        sumq_ref[:, cols] = (gq_block(a, b, c)[...].astype(F32) + rq_at(6, c)[...].astype(F32)).astype(BF16)
        store(sumq_ref.at[:, cols], sumq_out.at[:, cols])

    def go_rows(x_at, z_at, half=None):
        start = (x_at * 2 + z_at) * OROWS
        if half is None:
            return go.at[pl.ds(pl.multiple_of(start, OROWS), OROWS)]
        return go.at[pl.ds(pl.multiple_of(start + half * HALF, HALF), HALF)]

    def grad_out(g):
        rows = slice(2 * g * OROWS, 2 * (g + 1) * OROWS)

        @pl.loop(0, 2)
        def _(n):
            cols = rows_of(n, D // 2)
            go[rows, cols] = jnp.dot(att_t[rows, :], cot_ref[:, cols], preferred_element_type=F32).astype(BF16)

        send(go_rows(g, 1 - b), ro_z.at[g], rso_s.at[6 + g], rso_r.at[6 + g], across)

    def pair_out(step):
        x_at = at_x(step)
        got(ro_z.at[x_at], rso_r.at[6 + x_at])
        block = go_rows(x_at, b)
        block[...] = (block[...].astype(F32) + ro_z[x_at].astype(F32)).astype(BF16)

    def ring_out():
        pair_out(2)
        send(go_rows(at_x(2), b, 0), ro.at[0], rso_s.at[0], rso_r.at[0], left)
        send(go_rows(at_x(2), b, 1), ro.at[1], rso_s.at[1], rso_r.at[1], right)
        pair_out(3)
        send(go_rows(at_x(3), b, 1), ro.at[2], rso_s.at[2], rso_r.at[2], left)
        pair_out(1)
        send(go_rows(at_x(1), b, 0), ro.at[3], rso_s.at[3], rso_r.at[3], right)
        pair_out(0)

    def add_out():
        for n, (block, to) in enumerate(((go_rows(at_x(3), b, 0), left), (go_rows(at_x(1), b, 1), right))):
            got(ro.at[n], rso_r.at[n])
            block[...] = (block[...].astype(F32) + ro[n].astype(F32)).astype(BF16)
            send(block, ro.at[4 + n], rso_s.at[4 + n], rso_r.at[4 + n], to)

    def end_out():
        for n in range(2, 6):
            got(ro.at[n], rso_r.at[n])
        for half, (first, second) in enumerate(((3, 4), (2, 5))):
            sumo_ref[half * HALF : (half + 1) * HALF, :] = (
                go_rows(a, b, half)[...].astype(F32) + ro[first].astype(F32) + ro[second].astype(F32)
            ).astype(BF16)
        store(sumo_ref, sumo_out)

    def gain_grad():
        @pl.loop(0, 8)
        def _(j):
            dnormed = lax.dot_general(
                dm[...], wq[rows_of(j, QROWS), :], NT, preferred_element_type=F32
            ).astype(BF16).astype(F32)
            wide = x_ref[:, rows_of(j, QROWS)].astype(F32) * fac[...]
            g_rows[pl.ds(j, 1), :] = jnp.sum(dnormed * wide, axis=0, keepdims=True)

        @pl.loop(1, 8)
        def _(step):
            pltpu.make_async_remote_copy(
                src_ref=g_rows, dst_ref=g_recv.at[f], send_sem=gg_s.at[step], recv_sem=gg_r.at[step],
                device_id={"fsdp": lax.rem(f + step, 8)}, device_id_type=MESH,
            ).start()
        g_recv[f] = g_rows[...]

    def gain_sum():
        @pl.loop(1, 8)
        def _(step):
            got(g_recv.at[lax.rem(f - step + 8, 8)], gg_r.at[step])
        total = g_recv[0]
        for i in range(1, 8):
            total = total + g_recv[i]
        for i in range(8):
            sumg_ref[:, i * 256 : (i + 1) * 256] = total[i : i + 1, :]
        store(sumg_ref, sumg_out)

        @pl.loop(1, 8)
        def _(step):
            left_here(g_rows, gg_s.at[step])

    out_ringed.own()
    chunks[KCHUNK].own()
    out_paired.own()
    for copy in loads[:6]:
        copy.wait()
    island_start()
    normalise()
    chunks[VCHUNK].own()
    chunks[0].own()
    chunks[KCHUNK].pair()
    out_paired.pair()
    for copy in loads[6:]:
        copy.wait()
    out_ringed.onward()
    island_ring()
    chunks[KCHUNK].onward()
    chunks[VCHUNK].pair()
    chunks[0].pair()
    chunks[1].own()
    chunks[2].own()
    chunks[3].own()
    out_paired.onward()
    out_ringed.far()
    island_far()
    chunks[VCHUNK].onward()
    chunks[0].onward()
    chunks[KCHUNK].have()
    project(KCHUNK)
    island_sum()
    chunks[1].pair()
    chunks[2].pair()
    chunks[VCHUNK].have()
    project(VCHUNK)
    back_ring()
    chunks[3].onward()
    out_paired.have()
    out_ringed.have()
    project_back()
    chunks[0].have()
    project(0)
    back_core()
    attend(0)
    grad_chunk(0)
    chunks[1].onward()
    chunks[2].onward()
    chunks[3].far()
    grad_out(0)
    chunks[1].have()
    project(1)
    attend(1)
    grad_chunk(1)
    add_chunk(0)
    grad_out(1)
    chunks[2].have()
    project(2)
    attend(2)
    grad_chunk(2)
    add_chunk(1)
    grad_out(2)
    fold_chunk(0)
    chunks[3].have()
    project(3)
    attend(3)
    grad_chunk(3)
    grad_chunk(KCHUNK)
    grad_chunk(VCHUNK)
    add_chunk(2)
    grad_out(3)
    fold_chunk(1)
    add_chunk(3)
    fold_chunk(2)
    ring_out()
    add_chunk(KCHUNK)
    fold_chunk(3)
    add_chunk(VCHUNK)
    add_out()
    gain_grad()
    end_chunk(0)
    end_chunk(1)
    fold_chunk(KCHUNK)
    island_whole()
    fold_chunk(VCHUNK)
    end_chunk(2)
    end_chunk(3)
    end_out()
    end_chunk(KCHUNK)
    gain_sum()
    end_chunk(VCHUNK)
    for copy in stores:
        copy.wait()
    for src, s_sem in sent:
        left_here(src, s_sem)


def grads(islands, x, cot, gain, wq, wo, qglob, qmom, oglob, omom):
    qshare, oshare = QKV // islands, D // islands
    cosine, sine = rope_tables()
    hbm = pl.BlockSpec(memory_space=pl.ANY)
    dma = pltpu.SemaphoreType.DMA
    operands = (x, cot, gain, wq, wo, jnp.asarray(cosine), jnp.asarray(sine), qglob, qmom, oglob, omom)
    results = [
        jax.ShapeDtypeStruct((QROWS, QKV), BF16),
        jax.ShapeDtypeStruct((OROWS, D), BF16),
        jax.ShapeDtypeStruct((1, D), F32),
        jax.ShapeDtypeStruct((qshare, QROWS), F32),
        jax.ShapeDtypeStruct((OROWS, oshare), F32),
        jax.ShapeDtypeStruct((1, D), F32),
        jax.ShapeDtypeStruct((QROWS, QKV), BF16),
        jax.ShapeDtypeStruct((OROWS, D), BF16),
    ]
    return pl.pallas_call(
        functools.partial(grads_kernel, islands),
        out_shape=results,
        in_specs=[hbm] * 11,
        out_specs=[hbm] * 8,
        scratch_shapes=[
            *(pltpu.VMEM(operands[n].shape, operands[n].dtype) for n in (0, 1, 2, 5, 6, 7, 8, 9, 10)),
            *(pltpu.VMEM(r.shape, r.dtype) for r in results),
            pltpu.VMEM((D, QKV), BF16),
            pltpu.VMEM((QW, D), BF16),
            pltpu.VMEM((TOK, D), BF16),
            pltpu.VMEM((D, TOK), BF16),
            pltpu.VMEM((TOK, 1), F32),
            pltpu.VMEM((QKV, TOK), BF16),
            pltpu.VMEM((KV_HEADS, TOK, HEAD_DIM), BF16),
            pltpu.VMEM((KV_HEADS, TOK, HEAD_DIM), BF16),
            pltpu.VMEM((QW, TOK), BF16),
            pltpu.VMEM((QW, TOK), BF16),
            pltpu.VMEM((QKV, TOK), BF16),
            pltpu.VMEM((TOK, QKV), BF16),
            pltpu.VMEM((HEAD_DIM, TOK), F32),
            pltpu.VMEM((HEAD_DIM, TOK), F32),
            pltpu.VMEM((D, QKV), BF16),
            pltpu.VMEM((QW, D), BF16),
            pltpu.VMEM((7, QROWS, QKV), BF16),
            pltpu.VMEM((6, HALF, D), BF16),
            pltpu.VMEM((4, OROWS, D), BF16),
            pltpu.VMEM((8, 256), F32),
            pltpu.VMEM((8, 8, 256), F32),
            pltpu.VMEM((8, 2, qshare, QROWS), BF16),
            pltpu.VMEM((8, 2, OROWS, oshare), BF16),
            pltpu.VMEM((8, qshare, QROWS), BF16),
            pltpu.VMEM((8, OROWS, oshare), BF16),
            pltpu.VMEM((8, 256), F32),
            pltpu.VMEM((4, 2, qshare, QROWS), BF16),
            pltpu.VMEM((4, 2, OROWS, oshare), BF16),
            pltpu.VMEM((4, 8, 256), F32),
            pltpu.VMEM((qshare, QROWS), BF16),
            pltpu.VMEM((OROWS, oshare), BF16),
            pltpu.VMEM((8, 256), F32),
            pltpu.VMEM((8, 256), F32),
            pltpu.VMEM((8, 2, qshare, QROWS), BF16),
            pltpu.VMEM((8, 2, OROWS, oshare), BF16),
            dma((11,)),
            dma((13,)),
            dma((CHUNKS, 7)), dma((CHUNKS, 7)),
            dma((2, 9)), dma((2, 9)),
            dma((CHUNKS, 7)), dma((CHUNKS, 7)),
            dma((10,)), dma((10,)),
            dma((8,)), dma((8,)),
            dma((25,)), dma((25,)),
        ],
        compiler_params=pltpu.CompilerParams(
            collective_id=0, has_side_effects=True, vmem_limit_bytes=63 * 2**20
        ),
        name="grads",
    )(*operands)


PARTS = 2


def update_kernel(islands, *refs):
    (
        gain_ref, wq_in, wo_in, gf_ref, gs_ref, qf_in, qs_in, of_in, os_in,
        gg_ref, gm_ref, qg_ref, qm_ref, og_ref, om_ref,
        sumq_in, sumo_in, sumg_ref, totq_ref, toto_ref, totg_ref, wholeq_in, wholeo_in,
        gain_o, wq_out, wo_out, gf_o, gs_o, qf_out, qs_out, of_out, os_out,
        gg_o, gm_o, qg_o, qm_o, og_o, om_o,
        *scratch, in_sem, out_sem,
    ) = refs
    sources = (wq_in, sumq_in, qf_in, qs_in, wholeq_in, wo_in, sumo_in, of_in, os_in, wholeo_in)
    targets = (wq_out, qf_out, qs_out, wo_out, of_out, os_out)
    held, made = scratch[: len(sources)], scratch[len(sources) :]

    def part(ref, i):
        size = ref.shape[0] // PARTS
        return ref.at[pl.ds(i * size, size)]

    loads = [
        [pltpu.make_async_copy(part(src, i), part(dst, i), in_sem.at[i, n]) for n, (src, dst) in enumerate(zip(sources, held))]
        for i in range(PARTS)
    ]
    for row in loads:
        for copy in row:
            copy.start()
    scale = 1.0 / islands
    stepped, first, second = adamw(gain_ref[...], sumg_ref[...], gf_ref[...], gs_ref[...], 0.0)
    outer, momentum = nesterov(gg_ref[...], gm_ref[...], totg_ref[...] * scale)
    gain_o[...] = MIXING * stepped + (1.0 - MIXING) * outer
    gf_o[...] = first
    gs_o[...] = second
    gg_o[...] = outer
    gm_o[...] = momentum
    qg_o[...], qm_o[...] = nesterov(qg_ref[...], qm_ref[...], totq_ref[...] * scale)
    og_o[...], om_o[...] = nesterov(og_ref[...], om_ref[...], toto_ref[...] * scale)
    stores = []
    for i in range(PARTS):
        for copy in loads[i]:
            copy.wait()
        for which in range(2):
            w, s, m1, m2, whole = (part(ref, i) for ref in held[5 * which : 5 * which + 5])
            outs = [part(ref, i) for ref in made[3 * which : 3 * which + 3]]
            stepped, first, second = adamw(w[...], s[...].astype(F32), m1[...], m2[...], WEIGHT_DECAY)
            outs[0][...] = (MIXING * stepped + (1.0 - MIXING) * whole[...].astype(F32)).astype(BF16)
            outs[1][...] = first
            outs[2][...] = second
            for n in range(3):
                copy = pltpu.make_async_copy(
                    outs[n], part(targets[3 * which + n], i), out_sem.at[i, 3 * which + n]
                )
                copy.start()
                stores.append(copy)
    for copy in stores:
        copy.wait()


def update(islands, state, sums):
    def spec(array):
        big = array.shape in ((QROWS, QKV), (OROWS, D))
        return pl.BlockSpec(memory_space=pl.ANY if big else pltpu.VMEM)

    def room(*arrays):
        return [pltpu.VMEM(v.shape, v.dtype) for v in arrays]

    return pl.pallas_call(
        functools.partial(update_kernel, islands),
        out_shape=[jax.ShapeDtypeStruct(o.shape, o.dtype) for o in state],
        in_specs=[spec(v) for v in (*state, *sums)],
        out_specs=[spec(o) for o in state],
        scratch_shapes=[
            *room(state[1], sums[0], state[5], state[6], sums[6], state[2], sums[1], state[7], state[8], sums[7]),
            *room(state[1], state[5], state[6], state[2], state[7], state[8]),
            pltpu.SemaphoreType.DMA((PARTS, 10)),
            pltpu.SemaphoreType.DMA((PARTS, 6)),
        ],
        compiler_params=pltpu.CompilerParams(vmem_limit_bytes=60 * 2**20),
        name="update",
    )(*state, *sums)


def shards(
    tokens, cotangent, norm_gain, qkv_weight, out_weight, gain_first, gain_second,
    qkv_first, qkv_second, out_first, out_second,
    gain_global, gain_momentum, qkv_global, qkv_momentum, out_global, out_momentum,
):
    islands = lax.axis_size("island")
    wq, wo = qkv_weight[0], out_weight[0]
    qkv_global, qkv_momentum = qkv_global.T, qkv_momentum.T
    sums = grads(
        islands, tokens, cotangent, norm_gain, wq, wo, qkv_global, qkv_momentum, out_global, out_momentum
    )
    state = (
        norm_gain, wq, wo, gain_first, gain_second, qkv_first[0], qkv_second[0], out_first[0], out_second[0],
        gain_global[None], gain_momentum[None], qkv_global, qkv_momentum, out_global, out_momentum,
    )
    (
        gain_next, wq_next, wo_next, gf, gs, qf, qs, of, os_, gg, gm, qg, qm, og, om
    ) = update(islands, state, sums)
    return (
        gain_next, wq_next[None], wo_next[None], gf, gs, qf[None], qs[None], of[None], os_[None],
        gg[0], gm[0], qg.T, qm.T, og, om,
    )


def solution(mesh):
    placed = (
        P(("island", "fsdp"), None),
        P(("island", "fsdp"), None),
        P("island", None),
        P("island", "fsdp", None),
        P("island", "fsdp", None),
        P("island", None),
        P("island", None),
        P("island", "fsdp", None),
        P("island", "fsdp", None),
        P("island", "fsdp", None),
        P("island", "fsdp", None),
        P(),
        P(),
        P("fsdp", "island"),
        P("fsdp", "island"),
        P("fsdp", "island"),
        P("fsdp", "island"),
    )
    return jax.shard_map(
        shards,
        mesh=mesh,
        in_specs=placed,
        out_specs=(
            P("island", None),
            P("island", "fsdp", None),
            P("island", "fsdp", None),
            P("island", None),
            P("island", None),
            P("island", "fsdp", None),
            P("island", "fsdp", None),
            P("island", "fsdp", None),
            P("island", "fsdp", None),
            P(),
            P(),
            P("fsdp", "island"),
            P("fsdp", "island"),
            P("fsdp", "island"),
            P("fsdp", "island"),
        ),
        check_vma=False,
    )
```

```python
import functools

import jax
import jax.numpy as jnp
import numpy as np
from jax import lax
from jax.experimental import pallas as pl
from jax.experimental.pallas import tpu as pltpu
from jax.sharding import PartitionSpec as P

HEADS = 16
KV_HEADS = 4
HEAD_DIM = 64
GROUP = HEADS // KV_HEADS

BETA_ONE = 0.9
BETA_TWO = 0.95
ADAM_EPS = 1e-08
INNER_RATE = 0.001
WEIGHT_DECAY = 0.1
STEP_COUNT = 100.0
OUTER_RATE = 0.7
OUTER_MOMENTUM = 0.9
MIXING = 0.5
NORM_EPS = 1e-05
ROPE_BASE = 500000.0

MESH = pl.DeviceIdType.MESH
F32 = jnp.float32
BF16 = jnp.bfloat16

TOK = 512
D = 2048
QW = HEADS * HEAD_DIM
QKV = QW + 2 * KV_HEADS * HEAD_DIM
QROWS = 256
OROWS = 128
HALF = OROWS // 2
OPAIRED = 896
COLS = 256
CHUNKS = QKV // COLS
KCHUNK, VCHUNK = QW // COLS, QW // COLS + 1
QB = 512
NT = (((1,), (1,)), ((), ()))


def rope_tables():
    half = HEAD_DIM // 2
    freqs = ROPE_BASE ** (-np.arange(half, dtype=np.float64) / half)
    angles = freqs[:, None] * np.arange(TOK, dtype=np.float64)[None, :]
    return np.cos(angles).astype(np.float32), np.sin(angles).astype(np.float32)


def adamw(param, grad, first, second, decay):
    wide = param.astype(F32)
    first_next = BETA_ONE * first + (1.0 - BETA_ONE) * grad
    second_next = BETA_TWO * second + (1.0 - BETA_TWO) * grad * grad
    update = (
        first_next
        * (1.0 / (1.0 - BETA_ONE**STEP_COUNT))
        / (jnp.sqrt(second_next * (1.0 / (1.0 - BETA_TWO**STEP_COUNT))) + ADAM_EPS)
    )
    return (wide - INNER_RATE * (update + decay * wide), first_next, second_next)


def nesterov(global_value, momentum, average):
    delta = global_value - average
    momentum_next = OUTER_MOMENTUM * momentum + delta
    return (global_value - OUTER_RATE * (delta + OUTER_MOMENTUM * momentum_next), momentum_next)


def rows_of(index, size):
    return pl.ds(pl.multiple_of(index * size, size), size)


def grads_kernel(
    islands,
    x_in, cot_in, gain_in, wq_in, wo_in, cos_in, sin_in, qglob_in, qmom_in, oglob_in, omom_in,
    sumq_out, sumo_out, sumg_out, totq_out, toto_out, totg_out, wholeq_out, wholeo_out,
    x_ref, cot_ref, gain_ref, cos_ref, sin_ref, qglob_ref, qmom_ref, oglob_ref, omom_ref,
    sumq_ref, sumo_ref, sumg_ref, totq_ref, toto_ref, totg_ref, wholeq_ref, wholeo_ref,
    wq, wo, nrm, nrm_t, fac, qkv_t, k_tok, v_tok, datt_t, att_t, dm_t, dm, dk_acc, dv_acc,
    gq, go, rq, ro, ro_z, g_rows, g_recv,
    i_own, io_own, i_core, io_core, ig_core, i_ring, io_ring, ig_ring, i_far, io_far, ig_far, ig_own, i_back, io_back,
    own_sem, out_sem, agq_s, agq_r, ago_s, ago_r, rsq_s, rsq_r, rso_s, rso_r, gg_s, gg_r, is_s, is_r,
):
    f = lax.axis_index("fsdp")
    me = lax.axis_index("island")
    a, b = f // 2, f % 2
    y, zh, core = me // 4, (me // 2) % 2, me % 2
    qshare = QKV // islands
    oshare = D // islands

    def at_x(step):
        return lax.rem(a + step, 4)

    right = {"fsdp": at_x(1) * 2 + b}
    left = {"fsdp": at_x(3) * 2 + b}
    across = {"fsdp": a * 2 + 1 - b}
    sent = []

    def send(src, dst, s_sem, r_sem, to):
        copy = pltpu.make_async_remote_copy(
            src_ref=src, dst_ref=dst, send_sem=s_sem, recv_sem=r_sem, device_id=to, device_id_type=MESH
        )
        copy.start()
        sent.append((src, s_sem))

    def got(dst, r_sem):
        pltpu.make_async_remote_copy(
            src_ref=dst, dst_ref=dst, send_sem=r_sem, recv_sem=r_sem, device_id=across, device_id_type=MESH
        ).wait_recv()

    def left_here(src, s_sem):
        pltpu.make_async_remote_copy(
            src_ref=src, dst_ref=src, send_sem=s_sem, recv_sem=s_sem, device_id=across, device_id_type=MESH
        ).wait_send()

    barrier = pltpu.get_barrier_semaphore()

    @pl.loop(1, 8)
    def _(step):
        pl.semaphore_signal(barrier, inc=1, device_id={"fsdp": lax.rem(f + step, 8)}, device_id_type=MESH)

    other_core = {"island": me + 1 - 2 * core}
    other_far = {"island": me + 2 - 4 * zh}

    def other_y(step):
        return lax.rem(y + step, 4)

    def on_y(step):
        return {"island": other_y(step) * 4 + zh * 2 + core}

    pl.semaphore_signal(barrier, inc=1, device_id=other_core, device_id_type=MESH)
    pl.semaphore_signal(barrier, inc=1, device_id=other_far, device_id_type=MESH)
    for step in range(1, 4):
        pl.semaphore_signal(barrier, inc=1, device_id=on_y(step), device_id_type=MESH)
    loads = [
        pltpu.make_async_copy(src, dst, own_sem.at[n])
        for n, (src, dst) in enumerate((
            (x_in, x_ref), (gain_in, gain_ref), (wq_in, wq.at[rows_of(f, QROWS)]), (wo_in, wo.at[rows_of(f, OROWS)]),
            (cos_in, cos_ref), (sin_in, sin_ref), (cot_in, cot_ref), (qglob_in, qglob_ref), (qmom_in, qmom_ref),
            (oglob_in, oglob_ref), (omom_in, omom_ref),
        ))
    ]
    for copy in loads:
        copy.start()
    stores = []

    def store(src, dst):
        copy = pltpu.make_async_copy(src, dst, out_sem.at[len(stores)])
        copy.start()
        stores.append(copy)

    pl.semaphore_wait(barrier, 7 + 5)

    def wq_block(c):
        def block(x_at, z_at, half=None):
            start, size = (x_at * 2 + z_at) * QROWS, QROWS
            if half is not None:
                start, size = start + half * (QROWS // 2), QROWS // 2
            return wq.at[pl.ds(pl.multiple_of(start, size), size), pl.ds(c * COLS, COLS)]

        return block

    def wo_block(col, cols):
        def block(x_at, z_at, half=None):
            start, size = (x_at * 2 + z_at) * OROWS, OROWS
            if half is not None:
                start, size = start + half * HALF, HALF
            return wo.at[pl.ds(pl.multiple_of(start, size), size), pl.ds(col, cols)]

        return block

    class Paired:
        def __init__(self, src, block, n):
            self.src, self.block, self.s, self.r = src, block, agq_s.at[n], agq_r.at[n]

        def own(self):
            dst = self.block(a, b)
            send(self.src, dst, self.s.at[0], self.r.at[0], across)
            send(self.src, dst, self.s.at[1], self.r.at[1 + b], right)
            send(self.src, dst, self.s.at[2], self.r.at[3 + b], left)

        def pair(self):
            block = self.block(a, 1 - b)
            got(block, self.r.at[0])
            send(block, block, self.s.at[3], self.r.at[1 + 1 - b], right)
            send(block, block, self.s.at[4], self.r.at[3 + 1 - b], left)

        def onward(self):
            block = self.block(at_x(3), 1)
            got(block, self.r.at[2])
            send(block, block, self.s.at[5], self.r.at[5], right)
            block = self.block(at_x(1), 0)
            got(block, self.r.at[3])
            send(block, block, self.s.at[6], self.r.at[6], left)

        def have(self):
            got(self.block(at_x(3), 0), self.r.at[1])
            got(self.block(at_x(1), 1), self.r.at[4])
            got(self.block(at_x(2), 1), self.r.at[5])
            got(self.block(at_x(2), 0), self.r.at[6])

    class Ringed:
        def __init__(self, src, block, n):
            self.src, self.block, self.s, self.r = src, block, ago_s.at[n], ago_r.at[n]

        def own(self):
            dst = self.block(a, b)
            send(self.src, dst, self.s.at[0], self.r.at[0], right)
            send(self.src, dst, self.s.at[1], self.r.at[1], left)
            send(self.src, dst, self.s.at[2], self.r.at[2], across)

        def onward(self):
            for n, (x_at, to) in enumerate(((at_x(3), right), (at_x(1), left))):
                block, part = self.block(x_at, b), self.block(x_at, b, n)
                got(block, self.r.at[n])
                send(part, part, self.s.at[3 + n], self.r.at[3 + n], to)
                send(block, block, self.s.at[5 + n], self.r.at[5 + n], across)

        def far(self):
            for n in range(2):
                part = self.block(at_x(2), b, n)
                got(part, self.r.at[3 + n])
                send(part, part, self.s.at[7 + n], self.r.at[7 + n], across)

        def have(self):
            got(self.block(a, 1 - b), self.r.at[2])
            got(self.block(at_x(3), 1 - b), self.r.at[5])
            got(self.block(at_x(1), 1 - b), self.r.at[6])
            for n in range(2):
                got(self.block(at_x(2), 1 - b, n), self.r.at[7 + n])

    chunks = [
        (Paired if c != 3 else Ringed)(wq_in.at[:, pl.ds(c * COLS, COLS)], wq_block(c), c if c != 3 else 1)
        for c in range(CHUNKS)
    ]
    out_paired = Paired(wo_in.at[:, pl.ds(0, OPAIRED)], wo_block(0, OPAIRED), 3)
    out_ringed = Ringed(wo_in.at[:, pl.ds(OPAIRED, D - OPAIRED)], wo_block(OPAIRED, D - OPAIRED), 0)

    def island_start():
        own = wq.at[rows_of(f, QROWS)]
        for i in range(islands):
            if i % 4 == 0:
                turned = own[:, i * qshare : (i + 4) * qshare].astype(F32).T.astype(BF16)
            i_own[i // 2, i % 2] = turned[i % 4 * qshare : (i % 4 + 1) * qshare]
            io_own[i // 2, i % 2] = wo[rows_of(f, OROWS), i * oshare : (i + 1) * oshare]
        for i in range(8):
            ig_own[i : i + 1, :] = gain_ref[:, i * 256 : (i + 1) * 256]
        send(i_own.at[:, 1 - core], i_core, is_s.at[0], is_r.at[0], other_core)
        send(io_own.at[:, 1 - core], io_core, is_s.at[1], is_r.at[1], other_core)
        send(ig_own, ig_core, is_s.at[2], is_r.at[2], other_core)

    def island_ring():
        got(i_core, is_r.at[0])
        got(io_core, is_r.at[1])
        got(ig_core, is_r.at[2])

        @pl.loop(0, 8)
        def _(n):
            i_core[n] = (i_core[n].astype(F32) + i_own[n, core].astype(F32)).astype(BF16)
            io_core[n] = (io_core[n].astype(F32) + io_own[n, core].astype(F32)).astype(BF16)

        ig_core[...] += ig_own[...]
        for step in range(1, 4):
            two = pl.ds(other_y(step) * 2, 2)
            send(i_core.at[two], i_ring.at[y], is_s.at[3 * step], is_r.at[3 * step], on_y(step))
            send(io_core.at[two], io_ring.at[y], is_s.at[3 * step + 1], is_r.at[3 * step + 1], on_y(step))
            send(ig_core, ig_ring.at[y], is_s.at[3 * step + 2], is_r.at[3 * step + 2], on_y(step))
        two = pl.ds(y * 2, 2)
        i_ring[y] = i_core[two]
        io_ring[y] = io_core[two]
        ig_ring[y] = ig_core[...]

    def island_far():
        for step in range(1, 4):
            source = other_y(4 - step)
            got(i_ring.at[source], is_r.at[3 * step])
            got(io_ring.at[source], is_r.at[3 * step + 1])
            got(ig_ring.at[source], is_r.at[3 * step + 2])
        i_ring[0] = (
            i_ring[0].astype(F32) + i_ring[1].astype(F32) + i_ring[2].astype(F32) + i_ring[3].astype(F32)
        ).astype(BF16)
        io_ring[0] = (
            io_ring[0].astype(F32) + io_ring[1].astype(F32) + io_ring[2].astype(F32) + io_ring[3].astype(F32)
        ).astype(BF16)
        ig_ring[0] = ig_ring[0] + ig_ring[1] + ig_ring[2] + ig_ring[3]
        send(i_ring.at[0, 1 - zh], i_far, is_s.at[12], is_r.at[12], other_far)
        send(io_ring.at[0, 1 - zh], io_far, is_s.at[13], is_r.at[13], other_far)
        send(ig_ring.at[0], ig_far, is_s.at[14], is_r.at[14], other_far)

    def island_sum():
        got(i_far, is_r.at[12])
        got(io_far, is_r.at[13])
        got(ig_far, is_r.at[14])
        totq_ref[...] = i_ring[0, zh].astype(F32) + i_far[...].astype(F32)
        toto_ref[...] = io_ring[0, zh].astype(F32) + io_far[...].astype(F32)
        total = ig_ring[0] + ig_far[...]
        for i in range(8):
            totg_ref[:, i * 256 : (i + 1) * 256] = total[i : i + 1, :]
        here = me // 2
        i_back[here, core] = nesterov(
            qglob_ref[...], qmom_ref[...], totq_ref[...] * (1.0 / islands)
        )[0].astype(BF16)
        io_back[here, core] = nesterov(
            oglob_ref[...], omom_ref[...], toto_ref[...] * (1.0 / islands)
        )[0].astype(BF16)
        send(i_back.at[here, core], i_back.at[here, core], is_s.at[15], is_r.at[15], other_far)
        send(io_back.at[here, core], io_back.at[here, core], is_s.at[16], is_r.at[16], other_far)
        store(totq_ref, totq_out)
        store(toto_ref, toto_out)
        store(totg_ref, totg_out)

    def back_ring():
        there = y * 2 + 1 - zh
        got(i_back.at[there, core], is_r.at[15])
        got(io_back.at[there, core], is_r.at[16])
        mine = i_back.at[pl.ds(y * 2, 2), core], io_back.at[pl.ds(y * 2, 2), core]
        for step in range(1, 4):
            for n in range(2):
                at = 17 + 2 * (step - 1) + n
                send(mine[n], mine[n], is_s.at[at], is_r.at[at], on_y(step))

    def back_core():
        for step in range(1, 4):
            source = pl.ds(other_y(4 - step) * 2, 2)
            got(i_back.at[source, core], is_r.at[17 + 2 * (step - 1)])
            got(io_back.at[source, core], is_r.at[18 + 2 * (step - 1)])
        send(i_back.at[:, core], i_back.at[:, core], is_s.at[23], is_r.at[23], other_core)
        send(io_back.at[:, core], io_back.at[:, core], is_s.at[24], is_r.at[24], other_core)

    def island_whole():
        got(i_back.at[:, 1 - core], is_r.at[23])
        got(io_back.at[:, 1 - core], is_r.at[24])
        for i in range(islands // 4):
            four = jnp.concatenate([i_back[2 * i + n // 2, n % 2] for n in range(4)], axis=0)
            wholeq_ref[:, i * 4 * qshare : (i + 1) * 4 * qshare] = four.astype(F32).T.astype(BF16)
        for i in range(islands):
            wholeo_ref[:, i * oshare : (i + 1) * oshare] = io_back[i // 2, i % 2]
        store(wholeq_ref, wholeq_out)
        store(wholeo_ref, wholeo_out)

    def normalise():
        @pl.loop(0, TOK // 128)
        def _(t):
            rows = rows_of(t, 128)
            wide = x_ref[rows, :].astype(F32)
            factor = lax.rsqrt(jnp.mean(wide * wide, axis=-1, keepdims=True) + NORM_EPS)
            fac[rows, :] = factor
            normed = (wide * factor * gain_ref[...]).astype(BF16)
            nrm[rows, :] = normed
            nrm_t[:, rows] = normed.astype(F32).T.astype(BF16)

    def turn(first, second, sign):
        cosine, sine = cos_ref[...], sin_ref[...] * sign
        return first * cosine - second * sine, first * sine + second * cosine

    def project(c):
        mixed = jnp.dot(nrm[...], wq[:, c * COLS : (c + 1) * COLS], preferred_element_type=F32)
        if c == VCHUNK:
            mixed = mixed.astype(BF16).astype(F32)
        mixed_t = mixed.T
        for n in range(COLS // HEAD_DIM):
            at = n * HEAD_DIM
            head = mixed_t[at : at + HEAD_DIM, :]
            if c != VCHUNK:
                first, second = turn(head[: HEAD_DIM // 2], head[HEAD_DIM // 2 :], 1.0)
                head = jnp.concatenate([first, second], axis=0)
            held = head.astype(BF16)
            if c < KCHUNK:
                held = (held.astype(F32) * HEAD_DIM ** (-0.5)).astype(BF16)
            qkv_t[c * COLS + at : c * COLS + at + HEAD_DIM, :] = held
            if c == KCHUNK:
                k_tok[n] = held.astype(F32).T.astype(BF16)
            if c == VCHUNK:
                v_tok[n] = held.astype(F32).T.astype(BF16)

    def project_back():
        @pl.loop(0, 2)
        def _(j):
            rows = rows_of(j, QW // 2)
            datt_t[rows, :] = lax.dot_general(
                wo[rows, :], cot_ref[...], NT, preferred_element_type=F32
            ).astype(BF16)

    def attend(g):
        krows = slice(QW + g * HEAD_DIM, QW + (g + 1) * HEAD_DIM)
        vrows = slice(QW + (KV_HEADS + g) * HEAD_DIM, QW + (KV_HEADS + g + 1) * HEAD_DIM)
        dk_acc[...] = jnp.zeros_like(dk_acc)
        dv_acc[...] = jnp.zeros_like(dv_acc)

        @pl.loop(0, GROUP, unroll=4)
        def _(n):
            rows = rows_of(g * GROUP + n, HEAD_DIM)
            for q_at in range(0, TOK, QB):
                keys = q_at + QB
                queries = qkv_t[rows, q_at : q_at + QB]
                scores = jnp.dot(k_tok[g, :keys, :], queries, preferred_element_type=F32)
                key_at = lax.broadcasted_iota(jnp.int32, (QB, QB), 0)
                query_at = lax.broadcasted_iota(jnp.int32, (QB, QB), 1)
                masked = jnp.where(query_at >= key_at, scores[q_at:], -1e30)
                scores = jnp.concatenate([scores[:q_at], masked], axis=0) if q_at else masked
                top = jnp.max(scores, axis=0, keepdims=True)
                raised = jnp.exp(scores - top)
                soft = raised * (1.0 / jnp.sum(raised, axis=0, keepdims=True))
                weights = soft.astype(BF16)
                out = jnp.dot(qkv_t[vrows, :keys], weights, preferred_element_type=F32)
                att_t[rows, q_at : q_at + QB] = out.astype(BF16)
                dout = datt_t[rows, q_at : q_at + QB]
                dweights = jnp.dot(v_tok[g, :keys, :], dout, preferred_element_type=F32)
                dot_out = jnp.sum(out * dout.astype(F32), axis=0, keepdims=True)
                dscores = (soft * (dweights - dot_out)).astype(BF16)
                dqueries = jnp.dot(qkv_t[krows, :keys], dscores, preferred_element_type=F32)
                dqueries = (dqueries * HEAD_DIM ** (-0.5)).astype(BF16).astype(F32)
                half = HEAD_DIM // 2
                cosine, sine = cos_ref[:, q_at : q_at + QB], sin_ref[:, q_at : q_at + QB]
                first, second = dqueries[:half], dqueries[half:]
                dm_t[rows, q_at : q_at + QB] = jnp.concatenate(
                    [first * cosine + second * sine, second * cosine - first * sine], axis=0
                ).astype(BF16)
                dk_acc[:, :keys] += lax.dot_general(queries, dscores, NT, preferred_element_type=F32)
                dv_acc[:, :keys] += lax.dot_general(dout, weights, NT, preferred_element_type=F32)

        dkeys = dk_acc[...].astype(BF16).astype(F32)
        first, second = turn(dkeys[: HEAD_DIM // 2], dkeys[HEAD_DIM // 2 :], -1.0)
        dm_t[krows, :] = jnp.concatenate([first, second], axis=0).astype(BF16)
        dm_t[vrows, :] = dv_acc[...].astype(BF16)

    def gq_block(x_at, z_at, c):
        return gq.at[rows_of(x_at * 2 + z_at, QROWS), pl.ds(c * COLS, COLS)]

    def rq_at(n, c):
        return rq.at[n, :, pl.ds(c * COLS, COLS)]

    def grad_chunk(c):
        cols = slice(c * COLS, (c + 1) * COLS)

        dm[:, cols] = dm_t[cols, :].astype(F32).T.astype(BF16)

        @pl.loop(0, 2)
        def _(j):
            rows = rows_of(j, D // 2)
            gq[rows, cols] = jnp.dot(nrm_t[rows, :], dm[:, cols], preferred_element_type=F32).astype(BF16)

        for n, (block, to) in enumerate((
            (gq_block(at_x(2), 0, c), left),
            (gq_block(at_x(2), 1, c), right),
            (gq_block(at_x(3), 1, c), left),
            (gq_block(at_x(1), 0, c), right),
        )):
            send(block, rq_at(n, c), rsq_s.at[c, n], rsq_r.at[c, n], to)

    def add_chunk(c):
        for n, (block, to) in enumerate(((gq_block(at_x(3), 0, c), left), (gq_block(at_x(1), 1, c), right))):
            got(rq_at(n, c), rsq_r.at[c, n])
            block[...] = (block[...].astype(F32) + rq_at(n, c)[...].astype(F32)).astype(BF16)
            send(block, rq_at(4 + n, c), rsq_s.at[c, 4 + n], rsq_r.at[c, 4 + n], to)

    def fold_chunk(c):
        for n in range(2, 6):
            got(rq_at(n, c), rsq_r.at[c, n])

        def whole(z_at, first, second):
            return (
                gq_block(a, z_at, c)[...].astype(F32)
                + rq.at[first, :, pl.ds(c * COLS, COLS)][...].astype(F32)
                + rq.at[second, :, pl.ds(c * COLS, COLS)][...].astype(F32)
            )

        block = gq_block(a, 1 - b, c)
        block[...] = whole(1 - b, 2 + b, 5 - b).astype(BF16)
        send(block, rq_at(6, c), rsq_s.at[c, 6], rsq_r.at[c, 6], across)
        block = gq_block(a, b, c)
        block[...] = whole(b, 3 - b, 4 + b).astype(BF16)

    def end_chunk(c):
        got(rq_at(6, c), rsq_r.at[c, 6])
        cols = pl.ds(c * COLS, COLS)
        sumq_ref[:, cols] = (gq_block(a, b, c)[...].astype(F32) + rq_at(6, c)[...].astype(F32)).astype(BF16)
        store(sumq_ref.at[:, cols], sumq_out.at[:, cols])

    def go_rows(x_at, z_at, half=None):
        start = (x_at * 2 + z_at) * OROWS
        if half is None:
            return go.at[pl.ds(pl.multiple_of(start, OROWS), OROWS)]
        return go.at[pl.ds(pl.multiple_of(start + half * HALF, HALF), HALF)]

    def grad_out(g):
        rows = slice(2 * g * OROWS, 2 * (g + 1) * OROWS)

        @pl.loop(0, 2)
        def _(n):
            cols = rows_of(n, D // 2)
            go[rows, cols] = jnp.dot(att_t[rows, :], cot_ref[:, cols], preferred_element_type=F32).astype(BF16)

        send(go_rows(g, 1 - b), ro_z.at[g], rso_s.at[6 + g], rso_r.at[6 + g], across)

    def pair_out(step):
        x_at = at_x(step)
        got(ro_z.at[x_at], rso_r.at[6 + x_at])
        block = go_rows(x_at, b)
        block[...] = (block[...].astype(F32) + ro_z[x_at].astype(F32)).astype(BF16)

    def ring_out():
        pair_out(2)
        send(go_rows(at_x(2), b, 0), ro.at[0], rso_s.at[0], rso_r.at[0], left)
        send(go_rows(at_x(2), b, 1), ro.at[1], rso_s.at[1], rso_r.at[1], right)
        pair_out(3)
        send(go_rows(at_x(3), b, 1), ro.at[2], rso_s.at[2], rso_r.at[2], left)
        pair_out(1)
        send(go_rows(at_x(1), b, 0), ro.at[3], rso_s.at[3], rso_r.at[3], right)
        pair_out(0)

    def add_out():
        for n, (block, to) in enumerate(((go_rows(at_x(3), b, 0), left), (go_rows(at_x(1), b, 1), right))):
            got(ro.at[n], rso_r.at[n])
            block[...] = (block[...].astype(F32) + ro[n].astype(F32)).astype(BF16)
            send(block, ro.at[4 + n], rso_s.at[4 + n], rso_r.at[4 + n], to)

    def end_out():
        for n in range(2, 6):
            got(ro.at[n], rso_r.at[n])
        for half, (first, second) in enumerate(((3, 4), (2, 5))):
            sumo_ref[half * HALF : (half + 1) * HALF, :] = (
                go_rows(a, b, half)[...].astype(F32) + ro[first].astype(F32) + ro[second].astype(F32)
            ).astype(BF16)
        store(sumo_ref, sumo_out)

    def gain_grad():
        @pl.loop(0, 8)
        def _(j):
            dnormed = lax.dot_general(
                dm[...], wq[rows_of(j, QROWS), :], NT, preferred_element_type=F32
            ).astype(BF16).astype(F32)
            wide = x_ref[:, rows_of(j, QROWS)].astype(F32) * fac[...]
            g_rows[pl.ds(j, 1), :] = jnp.sum(dnormed * wide, axis=0, keepdims=True)

        @pl.loop(1, 8)
        def _(step):
            pltpu.make_async_remote_copy(
                src_ref=g_rows, dst_ref=g_recv.at[f], send_sem=gg_s.at[step], recv_sem=gg_r.at[step],
                device_id={"fsdp": lax.rem(f + step, 8)}, device_id_type=MESH,
            ).start()
        g_recv[f] = g_rows[...]

    def gain_sum():
        @pl.loop(1, 8)
        def _(step):
            got(g_recv.at[lax.rem(f - step + 8, 8)], gg_r.at[step])
        total = g_recv[0]
        for i in range(1, 8):
            total = total + g_recv[i]
        for i in range(8):
            sumg_ref[:, i * 256 : (i + 1) * 256] = total[i : i + 1, :]
        store(sumg_ref, sumg_out)

        @pl.loop(1, 8)
        def _(step):
            left_here(g_rows, gg_s.at[step])

    out_ringed.own()
    chunks[KCHUNK].own()
    out_paired.own()
    for copy in loads[:6]:
        copy.wait()
    island_start()
    normalise()
    chunks[VCHUNK].own()
    chunks[0].own()
    chunks[KCHUNK].pair()
    out_paired.pair()
    for copy in loads[6:]:
        copy.wait()
    out_ringed.onward()
    island_ring()
    chunks[KCHUNK].onward()
    chunks[VCHUNK].pair()
    chunks[0].pair()
    chunks[1].own()
    chunks[2].own()
    chunks[3].own()
    out_paired.onward()
    out_ringed.far()
    island_far()
    chunks[VCHUNK].onward()
    chunks[0].onward()
    chunks[KCHUNK].have()
    project(KCHUNK)
    island_sum()
    chunks[1].pair()
    chunks[2].pair()
    chunks[VCHUNK].have()
    project(VCHUNK)
    back_ring()
    chunks[3].onward()
    out_paired.have()
    out_ringed.have()
    project_back()
    chunks[0].have()
    project(0)
    back_core()
    attend(0)
    grad_chunk(0)
    chunks[1].onward()
    chunks[2].onward()
    chunks[3].far()
    grad_out(0)
    chunks[1].have()
    project(1)
    attend(1)
    grad_chunk(1)
    add_chunk(0)
    grad_out(1)
    chunks[2].have()
    project(2)
    attend(2)
    grad_chunk(2)
    add_chunk(1)
    grad_out(2)
    fold_chunk(0)
    chunks[3].have()
    project(3)
    attend(3)
    grad_chunk(3)
    grad_chunk(KCHUNK)
    grad_chunk(VCHUNK)
    add_chunk(2)
    grad_out(3)
    fold_chunk(1)
    add_chunk(3)
    fold_chunk(2)
    ring_out()
    add_chunk(KCHUNK)
    fold_chunk(3)
    add_chunk(VCHUNK)
    add_out()
    gain_grad()
    end_chunk(0)
    end_chunk(1)
    fold_chunk(KCHUNK)
    island_whole()
    fold_chunk(VCHUNK)
    end_chunk(2)
    end_chunk(3)
    end_out()
    end_chunk(KCHUNK)
    gain_sum()
    end_chunk(VCHUNK)
    for copy in stores:
        copy.wait()
    for src, s_sem in sent:
        left_here(src, s_sem)


def grads(islands, x, cot, gain, wq, wo, qglob, qmom, oglob, omom):
    qshare, oshare = QKV // islands, D // islands
    cosine, sine = rope_tables()
    hbm = pl.BlockSpec(memory_space=pl.ANY)
    dma = pltpu.SemaphoreType.DMA
    operands = (x, cot, gain, wq, wo, jnp.asarray(cosine), jnp.asarray(sine), qglob, qmom, oglob, omom)
    results = [
        jax.ShapeDtypeStruct((QROWS, QKV), BF16),
        jax.ShapeDtypeStruct((OROWS, D), BF16),
        jax.ShapeDtypeStruct((1, D), F32),
        jax.ShapeDtypeStruct((qshare, QROWS), F32),
        jax.ShapeDtypeStruct((OROWS, oshare), F32),
        jax.ShapeDtypeStruct((1, D), F32),
        jax.ShapeDtypeStruct((QROWS, QKV), BF16),
        jax.ShapeDtypeStruct((OROWS, D), BF16),
    ]
    return pl.pallas_call(
        functools.partial(grads_kernel, islands),
        out_shape=results,
        in_specs=[hbm] * 11,
        out_specs=[hbm] * 8,
        scratch_shapes=[
            *(pltpu.VMEM(operands[n].shape, operands[n].dtype) for n in (0, 1, 2, 5, 6, 7, 8, 9, 10)),
            *(pltpu.VMEM(r.shape, r.dtype) for r in results),
            pltpu.VMEM((D, QKV), BF16),
            pltpu.VMEM((QW, D), BF16),
            pltpu.VMEM((TOK, D), BF16),
            pltpu.VMEM((D, TOK), BF16),
            pltpu.VMEM((TOK, 1), F32),
            pltpu.VMEM((QKV, TOK), BF16),
            pltpu.VMEM((KV_HEADS, TOK, HEAD_DIM), BF16),
            pltpu.VMEM((KV_HEADS, TOK, HEAD_DIM), BF16),
            pltpu.VMEM((QW, TOK), BF16),
            pltpu.VMEM((QW, TOK), BF16),
            pltpu.VMEM((QKV, TOK), BF16),
            pltpu.VMEM((TOK, QKV), BF16),
            pltpu.VMEM((HEAD_DIM, TOK), F32),
            pltpu.VMEM((HEAD_DIM, TOK), F32),
            pltpu.VMEM((D, QKV), BF16),
            pltpu.VMEM((QW, D), BF16),
            pltpu.VMEM((7, QROWS, QKV), BF16),
            pltpu.VMEM((6, HALF, D), BF16),
            pltpu.VMEM((4, OROWS, D), BF16),
            pltpu.VMEM((8, 256), F32),
            pltpu.VMEM((8, 8, 256), F32),
            pltpu.VMEM((8, 2, qshare, QROWS), BF16),
            pltpu.VMEM((8, 2, OROWS, oshare), BF16),
            pltpu.VMEM((8, qshare, QROWS), BF16),
            pltpu.VMEM((8, OROWS, oshare), BF16),
            pltpu.VMEM((8, 256), F32),
            pltpu.VMEM((4, 2, qshare, QROWS), BF16),
            pltpu.VMEM((4, 2, OROWS, oshare), BF16),
            pltpu.VMEM((4, 8, 256), F32),
            pltpu.VMEM((qshare, QROWS), BF16),
            pltpu.VMEM((OROWS, oshare), BF16),
            pltpu.VMEM((8, 256), F32),
            pltpu.VMEM((8, 256), F32),
            pltpu.VMEM((8, 2, qshare, QROWS), BF16),
            pltpu.VMEM((8, 2, OROWS, oshare), BF16),
            dma((11,)),
            dma((13,)),
            dma((CHUNKS, 7)), dma((CHUNKS, 7)),
            dma((2, 9)), dma((2, 9)),
            dma((CHUNKS, 7)), dma((CHUNKS, 7)),
            dma((10,)), dma((10,)),
            dma((8,)), dma((8,)),
            dma((25,)), dma((25,)),
        ],
        compiler_params=pltpu.CompilerParams(
            collective_id=0, has_side_effects=True, vmem_limit_bytes=63 * 2**20
        ),
        name="grads",
    )(*operands)


SMALL = (0, 3, 4, 9, 10, 11, 12, 13, 14)
PARTS = 2


def update_kernel(islands, *refs):
    (
        gain_in, wq_in, wo_in, gf_in, gs_in, qf_in, qs_in, of_in, os_in,
        gg_in, gm_in, qg_in, qm_in, og_in, om_in,
        sumq_in, sumo_in, sumg_in, totq_in, toto_in, totg_in, wholeq_in, wholeo_in,
        gain_out, wq_out, wo_out, gf_out, gs_out, qf_out, qs_out, of_out, os_out,
        gg_out, gm_out, qg_out, qm_out, og_out, om_out,
        *scratch, in_sem, out_sem, small_in_sem, small_out_sem,
    ) = refs
    sources = (wq_in, sumq_in, qf_in, qs_in, wholeq_in, wo_in, sumo_in, of_in, os_in, wholeo_in)
    targets = (wq_out, qf_out, qs_out, wo_out, of_out, os_out)
    small_sources = (
        gain_in, gf_in, gs_in, gg_in, gm_in, qg_in, qm_in, og_in, om_in, sumg_in, totq_in, toto_in, totg_in
    )
    small_targets = (gain_out, gf_out, gs_out, gg_out, gm_out, qg_out, qm_out, og_out, om_out)
    scratch, small_made = scratch[:-9], scratch[-9:]
    scratch, small_held = scratch[:-13], scratch[-13:]
    gain_ref, gf_ref, gs_ref, gg_ref, gm_ref, qg_ref, qm_ref, og_ref, om_ref = small_held[:9]
    sumg_ref, totq_ref, toto_ref, totg_ref = small_held[9:]
    gain_o, gf_o, gs_o, gg_o, gm_o, qg_o, qm_o, og_o, om_o = small_made
    held, made = scratch[: len(sources)], scratch[len(sources) :]

    def part(ref, i):
        size = ref.shape[0] // PARTS
        return ref.at[pl.ds(i * size, size)]

    loads = [
        [pltpu.make_async_copy(part(src, i), part(dst, i), in_sem.at[i, n]) for n, (src, dst) in enumerate(zip(sources, held))]
        for i in range(PARTS)
    ]
    for row in loads:
        for copy in row:
            copy.start()
    small_loads = [
        pltpu.make_async_copy(src, dst, small_in_sem.at[n]) for n, (src, dst) in enumerate(zip(small_sources, small_held))
    ]
    for copy in small_loads:
        copy.start()
    for copy in small_loads:
        copy.wait()
    scale = 1.0 / islands
    stepped, first, second = adamw(gain_ref[...], sumg_ref[...], gf_ref[...], gs_ref[...], 0.0)
    outer, momentum = nesterov(gg_ref[...], gm_ref[...], totg_ref[...] * scale)
    gain_o[...] = MIXING * stepped + (1.0 - MIXING) * outer
    gf_o[...] = first
    gs_o[...] = second
    gg_o[...] = outer
    gm_o[...] = momentum
    qg_o[...], qm_o[...] = nesterov(qg_ref[...], qm_ref[...], totq_ref[...] * scale)
    og_o[...], om_o[...] = nesterov(og_ref[...], om_ref[...], toto_ref[...] * scale)
    stores = [
        pltpu.make_async_copy(src, dst, small_out_sem.at[n]) for n, (src, dst) in enumerate(zip(small_made, small_targets))
    ]
    for copy in stores:
        copy.start()
    for i in range(PARTS):
        for copy in loads[i]:
            copy.wait()
        for which in range(2):
            w, s, m1, m2, whole = (part(ref, i) for ref in held[5 * which : 5 * which + 5])
            outs = [part(ref, i) for ref in made[3 * which : 3 * which + 3]]
            stepped, first, second = adamw(w[...], s[...].astype(F32), m1[...], m2[...], WEIGHT_DECAY)
            outs[0][...] = (MIXING * stepped + (1.0 - MIXING) * whole[...].astype(F32)).astype(BF16)
            outs[1][...] = first
            outs[2][...] = second
            for n in range(3):
                copy = pltpu.make_async_copy(
                    outs[n], part(targets[3 * which + n], i), out_sem.at[i, 3 * which + n]
                )
                copy.start()
                stores.append(copy)
    for copy in stores:
        copy.wait()


def update(islands, state, sums):
    hbm = pl.BlockSpec(memory_space=pl.ANY)

    def room(*arrays):
        return [pltpu.VMEM(v.shape, v.dtype) for v in arrays]

    return pl.pallas_call(
        functools.partial(update_kernel, islands),
        out_shape=[jax.ShapeDtypeStruct(o.shape, o.dtype) for o in state],
        in_specs=[hbm] * (len(state) + len(sums)),
        out_specs=[hbm] * len(state),
        scratch_shapes=[
            *room(state[1], sums[0], state[5], state[6], sums[6], state[2], sums[1], state[7], state[8], sums[7]),
            *room(state[1], state[5], state[6], state[2], state[7], state[8]),
            *room(*(state[n] for n in SMALL), sums[2], sums[3], sums[4], sums[5]),
            *room(*(state[n] for n in SMALL)),
            pltpu.SemaphoreType.DMA((PARTS, 10)),
            pltpu.SemaphoreType.DMA((PARTS, 6)),
            pltpu.SemaphoreType.DMA((13,)),
            pltpu.SemaphoreType.DMA((9,)),
        ],
        compiler_params=pltpu.CompilerParams(vmem_limit_bytes=60 * 2**20),
        name="update",
    )(*state, *sums)


def shards(
    tokens, cotangent, norm_gain, qkv_weight, out_weight, gain_first, gain_second,
    qkv_first, qkv_second, out_first, out_second,
    gain_global, gain_momentum, qkv_global, qkv_momentum, out_global, out_momentum,
):
    islands = lax.axis_size("island")
    wq, wo = qkv_weight[0], out_weight[0]
    qkv_global, qkv_momentum = qkv_global.T, qkv_momentum.T
    sums = grads(
        islands, tokens, cotangent, norm_gain, wq, wo, qkv_global, qkv_momentum, out_global, out_momentum
    )
    state = (
        norm_gain, wq, wo, gain_first, gain_second, qkv_first[0], qkv_second[0], out_first[0], out_second[0],
        gain_global[None], gain_momentum[None], qkv_global, qkv_momentum, out_global, out_momentum,
    )
    (
        gain_next, wq_next, wo_next, gf, gs, qf, qs, of, os_, gg, gm, qg, qm, og, om
    ) = update(islands, state, sums)
    return (
        gain_next, wq_next[None], wo_next[None], gf, gs, qf[None], qs[None], of[None], os_[None],
        gg[0], gm[0], qg.T, qm.T, og, om,
    )


def solution(mesh):
    placed = (
        P(("island", "fsdp"), None),
        P(("island", "fsdp"), None),
        P("island", None),
        P("island", "fsdp", None),
        P("island", "fsdp", None),
        P("island", None),
        P("island", None),
        P("island", "fsdp", None),
        P("island", "fsdp", None),
        P("island", "fsdp", None),
        P("island", "fsdp", None),
        P(),
        P(),
        P("fsdp", "island"),
        P("fsdp", "island"),
        P("fsdp", "island"),
        P("fsdp", "island"),
    )
    return jax.shard_map(
        shards,
        mesh=mesh,
        in_specs=placed,
        out_specs=(
            P("island", None),
            P("island", "fsdp", None),
            P("island", "fsdp", None),
            P("island", None),
            P("island", None),
            P("island", "fsdp", None),
            P("island", "fsdp", None),
            P("island", "fsdp", None),
            P("island", "fsdp", None),
            P(),
            P(),
            P("fsdp", "island"),
            P("fsdp", "island"),
            P("fsdp", "island"),
            P("fsdp", "island"),
        ),
        check_vma=False,
    )
```
